128 devices in a mesh: dp: 8 (over x, core), tensor: 16 (over y, z).
Axes of the slice: x: 4, y: 4, z: 4, core: 2. Of those that a mesh axis runs over, the one named last changes fastest.
Arguments:
- hidden_input: bfloat16 [512, 8192], P('dp', 'tensor'), may hold values from -6 to 6
- query_projection_weight: bfloat16 [8192, 8192], P(None, 'tensor'), may hold values from -0.0625 to 0.0625
- key_projection_weight: bfloat16 [8192, 1024], P(None, 'tensor'), may hold values from -0.0625 to 0.0625
- value_projection_weight: bfloat16 [8192, 1024], P(None, 'tensor'), may hold values from -0.0625 to 0.0625
- adapter_down_maps: bfloat16 [512, 24, 8192], P(('dp', 'tensor')), may hold values from -0.0625 to 0.0625
- adapter_up_maps: bfloat16 [512, 8, 10240], P(('dp', 'tensor')), may hold values from -2 to 2
- key_cache_blocks: bfloat16 [16, 256, 512, 128], P('tensor', 'dp'), may hold values from -240 to 240
- value_cache_blocks: bfloat16 [16, 256, 512, 128], P('tensor', 'dp'), may hold values from -6 to 6
- filled: int32 [512], P('dp'), may hold values from 5 to 512, as said below
- positions: int32 [512], P('dp'), may hold values from 512 to 1023
- requests: int32 [8, 63], P('dp'), may hold values from 0 to 511, as said below
- session_request_slot: int32 [512], P('dp'), may hold values from 0 to 62, as said below
Outputs:
- attended: bfloat16 [512, 8192], P('dp', 'tensor')
- new_keys: bfloat16 [512, 1024], P('dp', 'tensor')
- fresh_values: bfloat16 [512, 1024], P('dp', 'tensor')
The draws below stay inside these ranges and needn't reach their ends.
Inputs may be any that keep to these rules, and one draw needn't show every extreme that they name: Slots below filled hold a session's keys and values, the 4 sinks first; at least one session uses all 512 slots. `requests`: A row lists 63 different adapters of one session group, no two on one device; adapter a lies on device a // 4 of dp+tensor. `session_request_slot`: every entry of a group's list is used; entry 0 by 2 sessions of the group, every other entry by 1.
All inputs are finite; a program needn't handle non-finite values.
Results may differ from the reference program's by a relative error of at most 0.012.
The reference program's roundings to bfloat16 on the way count: a program that leaves them out, or rounds other values in their place, can miss the bound.
Values may be sent and summed in bfloat16 or wider, within the bound.
No kernel may reach another device: no remote copies, remote signals or barrier semaphores. Data moves between devices by JAX's collectives and lax.ppermute only.
A program may use at most 128 MiB of HBM per device.

```python
import math
import jax
import jax.numpy as jnp
from jax import lax

MODEL_WIDTH = 8192
QUERY_HEADS = 64
KEY_HEADS = 8
HEAD_SIZE = 128
ADAPTER_RANK = 8
CACHE_SLOTS = 512
SINK = 4
SPE = 1
ADP_DEV = 4
REQ = 63
SESS_G = 64
SESSION_COUNT = 512
ADAPTER_COUNT = 512
SHARING_DEVICES = 2


def draw_key_cache_blocks(key, part):
    key = jax.random.fold_in(key, 11)
    cache_layout = (KEY_HEADS * SHARING_DEVICES, SESSION_COUNT // SHARING_DEVICES, CACHE_SLOTS, HEAD_SIZE)
    value_vectors = jnp.clip(jax.random.normal(key, cache_layout, jnp.float32), -6.0, 6.0)
    return value_vectors.astype(jnp.bfloat16)


def draw_filled(key, part):
    key = jax.random.fold_in(key, 9)
    lengths = jax.random.randint(key, (SESSION_COUNT,), SINK + 1, CACHE_SLOTS + 1)
    return lengths.at[0].set(CACHE_SLOTS).astype(jnp.int32)


def draw_requests(key, part):
    key = jax.random.fold_in(key, 5)
    holders = ADAPTER_COUNT // ADP_DEV
    group_count = SESSION_COUNT // SESS_G

    def per_group(group_key):
        perm_key, local_key = jax.random.split(group_key, 2)
        devices_used = jax.random.permutation(perm_key, holders)[:REQ]
        local_ids = jax.random.randint(local_key, (REQ,), 0, ADP_DEV)
        return devices_used * ADP_DEV + local_ids
    return jax.vmap(per_group)(jax.random.split(key, group_count)).astype(jnp.int32)


def draw_session_request_slot(key, part):
    key = jax.random.fold_in(key, 7)
    group_count = SESSION_COUNT // SESS_G
    slot_list = jnp.concatenate([jnp.repeat(jnp.arange(REQ, dtype=jnp.int32), SPE), jnp.zeros((SPE,), jnp.int32)])

    def per_group(group_key):
        return jax.random.permutation(group_key, slot_list)
    return jax.vmap(per_group)(jax.random.split(key, group_count)).reshape(SESSION_COUNT).astype(jnp.int32)


def place_ends(array, stream_key, smallest, high):
    dims = array.shape
    index_at = [jax.random.randint(jax.random.fold_in(stream_key, axis), (), 0, dims[axis]) for axis in range(len(dims))]
    array = array.at[tuple(index_at)].set(smallest)
    longest = dims.index(max(dims))
    index_at[longest] = (index_at[longest] + 1) % dims[longest]
    return array.at[tuple(index_at)].set(high)


def steps_of(key, dims, pieces, least, top_value):
    gain, own = 1.0, jax.random.fold_in(key, 6)
    for dim, parts in pieces:
        draws = jnp.exp(jax.random.uniform(jax.random.fold_in(own, dim), (parts,), jnp.float32, least / len(pieces), top_value / len(pieces)))
        gain = gain * jnp.repeat(draws, dims[dim] // parts).reshape([-1 if axis == dim else 1 for axis in range(len(dims))])
    return gain


def centred(rng, shape, spread, bound, cuts=(), kind=jnp.bfloat16):
    array = spread * jax.random.normal(rng, shape, jnp.float32)
    if cuts:
        array = array * steps_of(rng, shape, cuts, -0.22, 0.18)
    return jnp.clip(array, -bound, bound).astype(kind)


def setup_inputs(seed: int = 0) -> dict:
    splits = jax.random.split(jax.random.key(seed), 13)
    hidden_input = centred(splits[0], (SESSION_COUNT, MODEL_WIDTH), 1.0, 6.0, ((0, 8), (1, 16)))
    query_projection_weight = centred(splits[1], (MODEL_WIDTH, QUERY_HEADS * HEAD_SIZE), MODEL_WIDTH ** -0.5, 0.0625, ((1, 16),))
    key_projection_weight = centred(splits[2], (MODEL_WIDTH, KEY_HEADS * HEAD_SIZE), MODEL_WIDTH ** -0.5, 0.0625, ((1, 16),))
    value_projection_weight = centred(splits[3], (MODEL_WIDTH, KEY_HEADS * HEAD_SIZE), MODEL_WIDTH ** -0.5, 0.0625, ((1, 16),))
    adapter_down_maps = centred(splits[4], (ADAPTER_COUNT, 3 * ADAPTER_RANK, MODEL_WIDTH), MODEL_WIDTH ** -0.5, 0.0625, ((0, 128),))
    adapter_up_maps = centred(splits[5], (ADAPTER_COUNT, ADAPTER_RANK, QUERY_HEADS * HEAD_SIZE + 2 * KEY_HEADS * HEAD_SIZE), ADAPTER_RANK ** -0.5, 2.0, ((0, 128),))
    key_cache_blocks = draw_key_cache_blocks(jax.random.fold_in(splits[12], 71), 0)
    value_cache_blocks = centred(splits[7], (KEY_HEADS * SHARING_DEVICES, SESSION_COUNT // SHARING_DEVICES, CACHE_SLOTS, HEAD_SIZE), 1.0, 6.0, ((0, 16), (1, 8)))
    filled = draw_filled(jax.random.fold_in(splits[12], 71), 0)
    positions = place_ends(jax.random.randint(splits[9], (SESSION_COUNT,), CACHE_SLOTS, 2 * CACHE_SLOTS), jax.random.fold_in(splits[9], 1), CACHE_SLOTS, (2 * CACHE_SLOTS) - 1).astype(jnp.int32)
    requests = draw_requests(jax.random.fold_in(splits[12], 71), 0)
    session_request_slot = draw_session_request_slot(jax.random.fold_in(splits[12], 71), 0)
    return {"hidden_input": hidden_input, "query_projection_weight": query_projection_weight, "key_projection_weight": key_projection_weight, "value_projection_weight": value_projection_weight, "adapter_down_maps": adapter_down_maps, "adapter_up_maps": adapter_up_maps, "key_cache_blocks": key_cache_blocks, "value_cache_blocks": value_cache_blocks, "filled": filled, "positions": positions, "requests": requests, "session_request_slot": session_request_slot}


THETA = 500000.0

def apply_rotation(vector, positions_in):
    head_width = vector.shape[-1]
    half_width = head_width // 2
    frequency = THETA ** (-2.0 * jnp.arange(half_width, dtype=jnp.float32) / head_width)
    phase_angle = positions_in.astype(jnp.float32)[:, None, None] * frequency[None, None, :]
    cosine = jnp.cos(phase_angle)
    sine_part = jnp.sin(phase_angle)
    lower_half = vector[..., :half_width]
    upper_half = vector[..., half_width:]
    return jnp.concatenate([lower_half * cosine - upper_half * sine_part, upper_half * cosine + lower_half * sine_part], axis=-1)

def reference(hidden_input, query_projection_weight, key_projection_weight, value_projection_weight, adapter_down_maps, adapter_up_maps, key_cache_blocks, value_cache_blocks, filled, positions, requests, session_request_slot):
    group_of = jnp.arange(SESSION_COUNT, dtype=jnp.int32) // SESS_G
    adapter_index = requests[group_of, session_request_slot]
    mesh_coordinates = jnp.einsum('yu,ynu->yn', hidden_input.astype(jnp.float32), adapter_down_maps[adapter_index].astype(jnp.float32))
    mesh_coordinates = lax.optimization_barrier(mesh_coordinates.astype(jnp.bfloat16)).astype(jnp.float32)
    up_map_rows = adapter_up_maps[adapter_index].astype(jnp.float32)
    query_width = QUERY_HEADS * HEAD_SIZE
    key_value_width = KEY_HEADS * HEAD_SIZE
    low_query = jnp.einsum('sr,srn->sn', mesh_coordinates[:, :ADAPTER_RANK], up_map_rows[:, :, :query_width])
    low_key = jnp.einsum('sr,srn->sn', mesh_coordinates[:, ADAPTER_RANK:2 * ADAPTER_RANK], up_map_rows[:, :, query_width:query_width + key_value_width])
    low_value = jnp.einsum('sr,srn->sn', mesh_coordinates[:, 2 * ADAPTER_RANK:], up_map_rows[:, :, query_width + key_value_width:])
    query_pre = jnp.dot(hidden_input, query_projection_weight, preferred_element_type=jnp.float32) + low_query
    key_before_rotation = jnp.dot(hidden_input, key_projection_weight, preferred_element_type=jnp.float32) + low_key
    value_pre = jnp.dot(hidden_input, value_projection_weight, preferred_element_type=jnp.float32) + low_value
    query_rot = apply_rotation(query_pre.reshape(SESSION_COUNT, QUERY_HEADS, HEAD_SIZE), positions).astype(jnp.bfloat16)
    key_rotated = apply_rotation(key_before_rotation.reshape(SESSION_COUNT, KEY_HEADS, HEAD_SIZE), positions).astype(jnp.bfloat16)
    fresh_values = value_pre.astype(jnp.bfloat16)
    key_cache_view = key_cache_blocks.reshape(KEY_HEADS, SHARING_DEVICES, SESSION_COUNT // SHARING_DEVICES, CACHE_SLOTS, HEAD_SIZE)
    value_cache_view = value_cache_blocks.reshape(KEY_HEADS, SHARING_DEVICES, SESSION_COUNT // SHARING_DEVICES, CACHE_SLOTS, HEAD_SIZE)
    score_scale = 1.0 / math.sqrt(HEAD_SIZE)

    def attend(session_item):
        session_index, single_query, key_one, single_value, length = session_item
        parity = session_index % SHARING_DEVICES
        column = session_index // SHARING_DEVICES
        cached_keys = key_cache_view[:, parity, column].astype(jnp.float32)
        cached_values = value_cache_view[:, parity, column].astype(jnp.float32)
        grouped_queries = single_query.astype(jnp.float32).reshape(KEY_HEADS, QUERY_HEADS // KEY_HEADS, HEAD_SIZE)
        scores = jnp.einsum('hgd,hcd->hgc', grouped_queries, cached_keys) * score_scale
        own_score = jnp.einsum('hgd,hd->hg', grouped_queries, key_one.astype(jnp.float32)) * score_scale
        valid_slot = (jnp.arange(CACHE_SLOTS) < length)[None, None, :]
        top_score = jnp.maximum(lax.optimization_barrier(jnp.max(jnp.where(valid_slot, scores, -jnp.inf), axis=-1)), own_score)
        weights = jnp.where(valid_slot, jnp.exp(scores - top_score[..., None]), 0.0)
        own_weight = jnp.exp(own_score - top_score)
        denominator = lax.optimization_barrier(jnp.sum(weights, axis=-1)) + own_weight
        rounded = lax.optimization_barrier(weights.astype(jnp.bfloat16)).astype(jnp.float32)
        own_rounded_state = lax.optimization_barrier(own_weight.astype(jnp.bfloat16)).astype(jnp.float32)
        attention_output = jnp.einsum('hgc,hcd->hgd', rounded, cached_values)
        attention_output = attention_output + own_rounded_state[..., None] * single_value.astype(jnp.float32).reshape(KEY_HEADS, 1, HEAD_SIZE)
        return (attention_output / denominator[..., None]).reshape(QUERY_HEADS * HEAD_SIZE).astype(jnp.bfloat16)
    attended = lax.map(attend, (jnp.arange(SESSION_COUNT, dtype=jnp.int32), query_rot.reshape(SESSION_COUNT, QUERY_HEADS * HEAD_SIZE), key_rotated, fresh_values, filled))
    return (attended, key_rotated.reshape(SESSION_COUNT, KEY_HEADS * HEAD_SIZE), fresh_values)
```

```python
import functools
import math

import jax
import jax.numpy as jnp
from jax import lax
from jax.experimental import pallas as pl
from jax.experimental.pallas import tpu as pltpu
from jax.sharding import PartitionSpec as P

HEAD = 128
RANK = 8
THETA = 500000.0
ROUTE = ("tensor", "dp")
BF16 = jnp.bfloat16
F32 = jnp.float32


def owner_kernel(recv_ref, down_ref, up_ref, out_ref):
    acc = jnp.zeros((16, 96), F32)
    for t in range(16):
        acc = acc + lax.dot_general(
            recv_ref[t * 16 : (t + 1) * 16, 0:512],
            down_ref[:, t * 512 : (t + 1) * 512],
            (((1,), (1,)), ((), ())),
            preferred_element_type=F32,
        )
    ids = recv_ref[0:16, 512:640].astype(F32)[:, 0:1].astype(jnp.int32)
    coords = acc.astype(BF16).astype(F32)
    mine = lax.broadcasted_iota(jnp.int32, (16, 32), 1) // RANK == ids
    blocks = []
    for b in range(3):
        block = jnp.concatenate(
            [coords[:, a * 24 + b * 8 : a * 24 + b * 8 + 8] for a in range(4)], axis=1
        )
        blocks.append(jnp.where(mine, block, 0.0).astype(BF16))
    dot = functools.partial(jnp.dot, preferred_element_type=F32)
    low_key = dot(blocks[1], up_ref[:, 8192:9216])
    low_value = dot(blocks[2], up_ref[:, 9216:10240])
    for t in range(16):
        rows = slice(t * 16, (t + 1) * 16)
        head = slice((t // 2) * 128, (t // 2 + 1) * 128)
        out_ref[rows, 0:512] = dot(blocks[0], up_ref[:, t * 512 : (t + 1) * 512])
        out_ref[rows, 512:640] = low_key[:, head]
        out_ref[rows, 640:768] = low_value[:, head]


def owner_low(recv, down, up):
    return pl.pallas_call(
        owner_kernel,
        out_shape=jax.ShapeDtypeStruct((256, 768), F32),
        in_specs=[pl.BlockSpec(memory_space=pltpu.VMEM)] * 3,
        out_specs=pl.BlockSpec(memory_space=pltpu.VMEM),
        compiler_params=pltpu.CompilerParams(vmem_limit_bytes=16 * 2**20),
        cost_estimate=pl.CostEstimate(flops=40_000_000, bytes_accessed=3_400_000, transcendentals=0),
        name="owner_low",
    )(recv, down, up)


def base_kernel(order_ref, hidden_ref, wq_ref, wk_ref, wv_ref, q_ref, kv_ref):
    h = hidden_ref[0]
    q = jnp.dot(h, wq_ref[...], preferred_element_type=F32)
    nt = (((1,), (1,)), ((), ()))
    wkv = jnp.concatenate([wk_ref[...], wv_ref[...]], axis=0)
    kv = lax.dot_general(h, wkv, nt, preferred_element_type=F32)

    @pl.when(pl.program_id(0) == 0)
    def _():
        q_ref[...] = q
        kv_ref[...] = kv

    @pl.when(pl.program_id(0) != 0)
    def _():
        q_ref[...] += q
        kv_ref[...] += kv


def base_project(order, hidden, wq, wkt, wvt):
    return pl.pallas_call(
        base_kernel,
        grid_spec=pltpu.PrefetchScalarGridSpec(
            num_scalar_prefetch=1,
            grid=(16,),
            in_specs=[
                pl.BlockSpec((1, 64, 512), lambda i, o: (i, 0, 0)),
                pl.BlockSpec((512, 512), lambda i, o: (o[i], 0)),
                pl.BlockSpec((64, 512), lambda i, o: (0, o[i])),
                pl.BlockSpec((64, 512), lambda i, o: (0, o[i])),
            ],
            out_specs=[
                pl.BlockSpec((64, 512), lambda i, o: (0, 0)),
                pl.BlockSpec((64, 128), lambda i, o: (0, 0)),
            ],
        ),
        out_shape=[
            jax.ShapeDtypeStruct((64, 512), F32),
            jax.ShapeDtypeStruct((64, 128), F32),
        ],
        compiler_params=pltpu.CompilerParams(vmem_limit_bytes=16 * 2**20),
        cost_estimate=pl.CostEstimate(flops=671_000_000, bytes_accessed=11_700_000, transcendentals=0),
        name="base_project",
    )(order, hidden, wq, wkt, wvt)


def finish_kernel(
    piece_ref, parity_ref, low_ref, q_ref, kv_ref, cos_ref, sin_ref,
    mine_ref, give_ref, key_ref, value_ref, rows_ref,
):
    for i in range(64):
        rows_ref[i : i + 1, :] = low_ref[pl.ds(piece_ref[i], 1), :]

    def rotate(part, cos, sin):
        return part * cos + pltpu.roll(part, 64, 1) * sin

    cos, sin = cos_ref[...], sin_ref[...]
    key_ref[...] = rotate(kv_ref[:, 0:128] + rows_ref[:, 512:640], cos, sin).astype(BF16)
    value_ref[...] = (kv_ref[:, 128:256] + rows_ref[:, 640:768]).astype(BF16)
    parity = parity_ref[0]
    for ref, which in ((mine_ref, parity), (give_ref, 1 - parity)):
        rows = pl.ds(pl.multiple_of(which * 32, 32), 32)
        cos, sin = cos_ref[rows, :], sin_ref[rows, :]
        for h in range(4):
            cols = slice(h * 128, (h + 1) * 128)
            ref[:, cols] = rotate(q_ref[rows, cols] + rows_ref[rows, cols], cos, sin).astype(BF16)


def finish(piece, parity, low, q, kv, cos, sin):
    smem, vmem = pl.BlockSpec(memory_space=pltpu.SMEM), pl.BlockSpec(memory_space=pltpu.VMEM)
    return pl.pallas_call(
        finish_kernel,
        out_shape=[
            jax.ShapeDtypeStruct((32, 512), BF16),
            jax.ShapeDtypeStruct((32, 512), BF16),
            jax.ShapeDtypeStruct((64, 128), BF16),
            jax.ShapeDtypeStruct((64, 128), BF16),
        ],
        in_specs=[smem, smem] + [vmem] * 5,
        out_specs=[vmem] * 4,
        scratch_shapes=[pltpu.VMEM((64, 768), F32)],
        compiler_params=pltpu.CompilerParams(vmem_limit_bytes=16 * 2**20),
        cost_estimate=pl.CostEstimate(flops=1_000_000, bytes_accessed=1_200_000, transcendentals=0),
        name="finish",
    )(piece, parity, low, q, kv, cos, sin)


def attend_block(query_rot, key_new, value_new, key_rows, value_rows, length):
    scale = 1.0 / math.sqrt(HEAD)
    scores = jnp.einsum("sgd,scd->sgc", query_rot, key_rows, preferred_element_type=F32) * scale
    own = jnp.einsum("sgd,sd->sg", query_rot, key_new, preferred_element_type=F32) * scale
    valid = (jnp.arange(key_rows.shape[1])[None, :] < length[:, None])[:, None, :]
    top = jnp.maximum(jnp.max(jnp.where(valid, scores, -jnp.inf), axis=-1), own)
    weights = jnp.where(valid, jnp.exp(scores - top[..., None]), 0.0)
    own_weight = jnp.exp(own - top)
    total = jnp.sum(weights, axis=-1) + own_weight
    out = jnp.einsum("sgc,scd->sgd", weights.astype(BF16), value_rows, preferred_element_type=F32)
    own_rounded = lax.optimization_barrier(own_weight.astype(BF16)).astype(F32)
    out = out + own_rounded[..., None] * value_new.astype(F32)[:, None, :]
    return (out / total[..., None]).astype(BF16)


def local(
    hidden, wq, wk, wv, down_maps, up_maps, key_cache, value_cache, filled, positions, requests, slots
):
    t = lax.axis_index("tensor")
    parity = t % 2
    z, y = t % 4, t // 4

    def z_turn(k):
        return [(4 * a + b, 4 * a + (b + k) % 4) for a in range(4) for b in range(4)]

    def y_turn(k):
        return [(4 * a + b, 4 * ((a + k) % 4) + b) for a in range(4) for b in range(4)]

    swap = [(i, i ^ 1) for i in range(16)]

    match = slots[:, None] == jnp.arange(63)[None, :]
    adapter = jnp.sum(jnp.where(match, requests, 0), axis=1)
    owner = adapter // 4
    earlier = jnp.arange(64)[None, :] < jnp.arange(64)[:, None]
    second = jnp.any(earlier & (slots[:, None] == slots[None, :]), axis=1)
    piece = ((owner % 16) * 8 + owner // 16) * 2 + second.astype(jnp.int32)
    place = (jnp.arange(256)[:, None] == piece[None, :]).astype(BF16)
    ids = jnp.broadcast_to((adapter % 4).astype(BF16)[:, None], (64, 128))
    sent = jnp.dot(place, jnp.concatenate([hidden, ids], axis=1), preferred_element_type=F32)
    sent = sent.astype(BF16).reshape(128, 2, 640)

    def evens_first(x):
        return jnp.swapaxes(x.reshape((32, 2) + x.shape[1:]), 0, 1)

    split = evens_first(hidden).reshape(64, 512)
    around_z = [split] + [lax.ppermute(split, "tensor", z_turn(k)) for k in (1, 2, 3)]
    recv = lax.all_to_all(sent, ROUTE, 0, 0, tiled=True)
    band = jnp.stack(around_z)
    around_y = [band] + [lax.ppermute(band, "tensor", y_turn(k)) for k in (1, 2, 3)]

    low_sent = owner_low(
        recv.reshape(256, 640), down_maps.reshape(96, 8192), up_maps.reshape(32, 10240)
    )
    low = lax.all_to_all(low_sent.reshape(128, 2, 768), ROUTE, 0, 0, tiled=True)

    blocks = jnp.concatenate(around_y)
    turns = jnp.arange(16)
    order = 4 * ((y - turns // 4) % 4) + (z - turns % 4) % 4
    base_q, base_kv = base_project(order.astype(jnp.int32), blocks, wq, wk.T, wv.T)
    other_kv = lax.ppermute(base_kv, "tensor", swap)
    first = jnp.where(parity == 0, base_kv, other_kv)
    last = jnp.where(parity == 0, other_kv, base_kv)
    full_kv = jnp.concatenate(
        [first[:, :64], last[:, :64], first[:, 64:], last[:, 64:]], axis=1
    )

    pos = evens_first(positions).reshape(64)
    freq = THETA ** (-2.0 * jnp.arange(64, dtype=F32) / HEAD)
    angle = pos.astype(F32)[:, None] * freq[None, :]
    cos, sin = jnp.cos(angle), jnp.sin(angle)
    cos, sin = jnp.concatenate([cos, cos], 1), jnp.concatenate([-sin, sin], 1)
    q_mine, q_give, key_all, value_all = finish(
        evens_first(piece).reshape(64), parity.reshape(1), low.reshape(256, 768), base_q, full_kv, cos, sin
    )
    q_got = lax.ppermute(q_give, "tensor", swap)
    is_even = parity == 0
    query = jnp.where(
        is_even,
        jnp.concatenate([q_mine, q_got], axis=1),
        jnp.concatenate([q_got, q_mine], axis=1),
    ).reshape(32, 8, HEAD)

    def interleave(x):
        return jnp.swapaxes(x.reshape(2, 32, -1), 0, 1).reshape(64, -1)

    def my_half(x):
        return interleave(jnp.where(is_even, x[:, :64], x[:, 64:]))

    new_keys, fresh = my_half(key_all), my_half(value_all)
    key_mine = lax.dynamic_slice_in_dim(key_all, parity * 32, 32, 0)
    value_mine = lax.dynamic_slice_in_dim(value_all, parity * 32, 32, 0)
    filled_mine = lax.dynamic_index_in_dim(filled.reshape(32, 2), parity, 1, keepdims=False)
    out = attend_block(query, key_mine, value_mine, key_cache[0], value_cache[0], filled_mine)
    out = out.reshape(32, 1024)
    own = jnp.where(is_even, out[:, :512], out[:, 512:])
    give = jnp.where(is_even, out[:, 512:], out[:, :512])
    back = lax.ppermute(give, "tensor", swap)
    attended = jnp.where(
        is_even, jnp.stack([own, back], axis=1), jnp.stack([back, own], axis=1)
    ).reshape(64, 512)
    return attended, new_keys, fresh


def solution(mesh):
    return jax.shard_map(
        local,
        mesh=mesh,
        in_specs=(
            P("dp", "tensor"),
            P(None, "tensor"),
            P(None, "tensor"),
            P(None, "tensor"),
            P(("dp", "tensor"), None, None),
            P(("dp", "tensor"), None, None),
            P("tensor", "dp", None, None),
            P("tensor", "dp", None, None),
            P("dp"),
            P("dp"),
            P("dp", None),
            P("dp"),
        ),
        out_specs=(P("dp", "tensor"), P("dp", "tensor"), P("dp", "tensor")),
        check_vma=False,
    )
```

```python
import functools
import math

import jax
import jax.numpy as jnp
from jax import lax
from jax.experimental import pallas as pl
from jax.experimental.pallas import tpu as pltpu
from jax.sharding import PartitionSpec as P

HEAD = 128
RANK = 8
THETA = 500000.0
ROUTE = ("tensor", "dp")
BF16 = jnp.bfloat16
F32 = jnp.float32
SMEM = pl.BlockSpec(memory_space=pltpu.SMEM)
VMEM = pl.BlockSpec(memory_space=pltpu.VMEM)
ANY = pl.BlockSpec(memory_space=pl.ANY)
NT = (((1,), (1,)), ((), ()))
dot = functools.partial(jnp.dot, preferred_element_type=F32)
dot_nt = functools.partial(lax.dot_general, dimension_numbers=NT, preferred_element_type=F32)


def prepare_kernel(
    requests_hbm, slots_hbm, hidden_hbm, sent_ref, plan_ref,
    rows_ref, wide_ref, hidden_ref, requests_ref, slots_ref, sems,
):
    copies = [
        pltpu.make_async_copy(requests_hbm, requests_ref, sems.at[0]),
        pltpu.make_async_copy(slots_hbm, slots_ref, sems.at[1]),
        pltpu.make_async_copy(hidden_hbm, hidden_ref, sems.at[2]),
    ]
    for copy in copies:
        copy.start()
    rows_ref[...] = jnp.zeros_like(rows_ref)
    for copy in copies:
        copy.wait()
    wide_ref[:, 0:512] = hidden_ref[...].astype(F32)
    first = jnp.int32(-1)
    last = jnp.int32(-1)
    for s in range(64):
        slot = slots_ref[s]
        adapter = requests_ref[0, slot]
        owner = adapter >> 2
        place = (owner & 15) * 8 + (owner >> 4)
        plan_ref[s] = place
        zero = slot == 0
        rank = jnp.where(zero & (first >= 0), 1, 0)
        last = jnp.where(zero, s, last)
        first = jnp.where(zero & (first < 0), s, first)
        code = ((adapter & 3) + 4 * (s % 2)).astype(F32)
        wide_ref[s : s + 1, 512:640] = jnp.full((1, 128), code, F32)
        rows_ref[place, pl.ds(rank, 1), :] = wide_ref[s : s + 1, :]
    plan_ref[64] = first
    plan_ref[65] = last
    sent_ref[...] = rows_ref[...].astype(BF16)


def in_hbm(*arrays):
    return [pltpu.with_memory_space_constraint(x, pltpu.HBM) for x in arrays]


def prepare(requests, slots, hidden):
    return pl.pallas_call(
        prepare_kernel,
        out_shape=[
            jax.ShapeDtypeStruct((128, 2, 640), BF16),
            jax.ShapeDtypeStruct((66,), jnp.int32),
        ],
        in_specs=[ANY] * 3,
        out_specs=[VMEM, SMEM],
        scratch_shapes=[
            pltpu.VMEM((128, 2, 640), F32),
            pltpu.VMEM((64, 640), F32),
            pltpu.VMEM((64, 512), BF16),
            pltpu.SMEM((1, 63), jnp.int32),
            pltpu.SMEM((64,), jnp.int32),
            pltpu.SemaphoreType.DMA((3,)),
        ],
        cost_estimate=pl.CostEstimate(flops=1_000_000, bytes_accessed=500_000, transcendentals=0),
        compiler_params=pltpu.CompilerParams(vmem_limit_bytes=4 * 2**20),
        name="prepare",
    )(*in_hbm(requests, slots, hidden))


def owner_kernel(recv_ref, down_hbm, up_hbm, out_ref, down_ref, up_ref, coords_ref, code_ref, sems):
    parts = [
        pltpu.make_async_copy(
            down_hbm.at[:, i * 2048 : (i + 1) * 2048], down_ref.at[:, i * 2048 : (i + 1) * 2048], sems.at[i]
        )
        for i in range(4)
    ]
    copy = pltpu.make_async_copy(up_hbm, up_ref, sems.at[4])
    for part in parts:
        part.start()
    copy.start()
    acc = jnp.zeros((16, 96), F32)
    for t in range(16):
        if t % 4 == 0:
            parts[t // 4].wait()
        acc = acc + dot_nt(
            recv_ref[t * 8 : (t + 1) * 8, :, 0:512].reshape(16, 512),
            down_ref[:, t * 512 : (t + 1) * 512],
        )
    coords_ref[:, 0:96] = acc.astype(BF16).astype(F32)
    code_ref[...] = recv_ref[0:8, :, 512:640].reshape(16, 128).astype(F32)
    one, two = coords_ref[pl.ds(0, 8, 2), :], coords_ref[pl.ds(1, 8, 2), :]
    code = code_ref[pl.ds(0, 8, 2), :][:, 0:1].astype(jnp.int32)
    odd = code >= 4
    coords = jnp.concatenate([jnp.where(odd, two, one), jnp.where(odd, one, two)], axis=0)
    ids = jnp.concatenate([code, code], axis=0) & 3
    mine = (lax.broadcasted_iota(jnp.int32, (16, 32), 1) >> 3) == ids
    blocks = []
    for b in range(3):
        block = jnp.concatenate(
            [coords[:, a * 24 + b * 8 : a * 24 + b * 8 + 8] for a in range(4)], axis=1
        )
        blocks.append(jnp.where(mine, block, 0.0).astype(BF16))
    copy.wait()
    low_key = dot(blocks[1], up_ref[:, 8192:9216])
    low_value = dot(blocks[2], up_ref[:, 9216:10240])
    for j in range(8):
        low_query = dot(blocks[0], up_ref[:, j * 1024 : (j + 1) * 1024])
        head = slice(j * 128, (j + 1) * 128)
        for p in range(2):
            rows, half = slice((2 * j + p) * 8, (2 * j + p + 1) * 8), slice(p * 8, p * 8 + 8)
            out_ref[rows, 0, 0:1024] = low_query[half]
            out_ref[rows, 0, 1024:1152] = low_key[half, head]
            out_ref[rows, 0, 1152:1280] = low_value[half, head]


def owner_low(recv, down, up):
    return pl.pallas_call(
        owner_kernel,
        out_shape=jax.ShapeDtypeStruct((128, 1, 1280), F32),
        in_specs=[VMEM, ANY, ANY],
        out_specs=VMEM,
        scratch_shapes=[
            pltpu.VMEM((96, 8192), BF16),
            pltpu.VMEM((32, 10240), BF16),
            pltpu.VMEM((16, 128), F32),
            pltpu.VMEM((16, 128), F32),
            pltpu.SemaphoreType.DMA((5,)),
        ],
        cost_estimate=pl.CostEstimate(flops=40_000_000, bytes_accessed=3_400_000, transcendentals=0),
        compiler_params=pltpu.CompilerParams(vmem_limit_bytes=8 * 2**20),
        name="owner_low",
    )(recv, *in_hbm(down, up))


def base_kernel(
    order_ref, plan_ref, h0_ref, h1_ref, h2_ref, h3_ref, wq_hbm, wk_hbm, wv_hbm, key_hbm, value_hbm, _,
    mine_ref, give_ref, key2_ref, value2_ref, wq_ref, wk_ref, wv_ref, acc_ref, sems,
):
    order = [order_ref[i] * 512 for i in range(16)]
    parity = order_ref[16]
    kv = [
        pltpu.make_async_copy(wk_hbm, wk_ref, sems.at[16]),
        pltpu.make_async_copy(wv_hbm, wv_ref, sems.at[17]),
    ]
    cache = [
        pltpu.make_async_copy(key_hbm.at[plan_ref[65] >> 1], key2_ref, sems.at[18]),
        pltpu.make_async_copy(value_hbm.at[plan_ref[65] >> 1], value2_ref, sems.at[19]),
    ]
    blocks = [
        pltpu.make_async_copy(
            wq_hbm.at[pl.ds(pl.multiple_of(order[i], 512), 512), :], wq_ref.at[i], sems.at[i]
        )
        for i in range(16)
    ]
    for copy in kv + blocks + cache:
        copy.start()
    for copy in kv:
        copy.wait()
    q = jnp.zeros((64, 512), F32)
    for i in range(16):
        h = (h0_ref, h1_ref, h2_ref, h3_ref)[i // 4][i % 4]
        cols = pl.ds(pl.multiple_of(order[i], 512), 512)
        wkv = jnp.concatenate([wk_ref[:, cols], wv_ref[:, cols]], axis=0)
        kv_part = dot_nt(h, wkv)
        if i == 0:
            acc_ref[:, 512:640] = kv_part
        else:
            acc_ref[:, 512:640] += kv_part
        blocks[i].wait()
        if i == 0:
            acc_ref[:, 0:512] = dot(h, wq_ref[i])
        else:
            acc_ref[:, 0:512] += dot(h, wq_ref[i])
    mine_ref[...] = acc_ref[pl.ds(pl.multiple_of(parity * 32, 32), 32), :]
    give_ref[...] = acc_ref[pl.ds(pl.multiple_of((1 - parity) * 32, 32), 32), :]
    for copy in cache:
        copy.wait()


def base_project(order, plan, bands, wq, wkt, wvt, keys, values, after):
    return pl.pallas_call(
        base_kernel,
        out_shape=[
            jax.ShapeDtypeStruct((32, 640), F32),
            jax.ShapeDtypeStruct((32, 640), F32),
            jax.ShapeDtypeStruct(keys.shape[1:], BF16),
            jax.ShapeDtypeStruct(values.shape[1:], BF16),
        ],
        in_specs=[SMEM] * 2 + [VMEM] * 4 + [ANY] * 6,
        out_specs=[VMEM] * 4,
        scratch_shapes=[
            pltpu.VMEM((16, 512, 512), BF16),
            pltpu.VMEM((64, 8192), BF16),
            pltpu.VMEM((64, 8192), BF16),
            pltpu.VMEM((64, 640), F32),
            pltpu.SemaphoreType.DMA((20,)),
        ],
        cost_estimate=pl.CostEstimate(flops=671_000_000, bytes_accessed=11_700_000, transcendentals=0),
        compiler_params=pltpu.CompilerParams(vmem_limit_bytes=16 * 2**20),
        name="base_project",
    )(order, plan, *bands, *in_hbm(wq, wkt, wvt, keys, values), after)


def rotate(part, cos, sin):
    return part * cos + pltpu.roll(part, 64, 1) * sin


def attend(query, key_new, value_new, keys, values, used):
    scale = 1.0 / math.sqrt(HEAD)
    scores = dot_nt(query.astype(BF16), keys) * scale
    own = jnp.sum(query * key_new, axis=1, keepdims=True) * scale
    valid = lax.broadcasted_iota(jnp.int32, scores.shape, 1) < used
    top = jnp.max(jnp.where(valid, scores, -jnp.inf), axis=1, keepdims=True)
    top = jnp.maximum(top, own)
    weights = jnp.where(valid, jnp.exp(scores - top), 0.0)
    own_weight = jnp.exp(own - top)
    total = jnp.sum(weights, axis=1, keepdims=True) + own_weight
    out = dot(weights.astype(BF16), values) + own_weight.astype(BF16).astype(F32) * value_new
    return out / total


def sides(parity, mine, other):
    even = parity == 0
    return jnp.where(even, mine, other), jnp.where(even, other, mine)


def project(parity, mine, other, low, cos, sin):
    def rounded(x):
        return x.astype(BF16).astype(F32)

    left, right = sides(parity, mine, other)
    heads = []
    for h in range(8):
        base = (left if h < 4 else right)[:, (h % 4) * 128 : (h % 4 + 1) * 128]
        heads.append(rounded(rotate(base + low[:, h * 128 : (h + 1) * 128], cos, sin)))
    key = jnp.concatenate([left[:, 512:576], right[:, 512:576]], axis=1) + low[:, 1024:1152]
    value = jnp.concatenate([left[:, 576:640], right[:, 576:640]], axis=1) + low[:, 1152:1280]
    return heads, rounded(rotate(key, cos, sin)), rounded(value)


def split(parity, outs, key, value):
    low = jnp.concatenate(outs[:4] + [key[:, :64], value[:, :64]], axis=1)
    high = jnp.concatenate(outs[4:] + [key[:, 64:], value[:, 64:]], axis=1)
    return sides(parity, low, high)


def attend_kernel(
    plan_ref, parity_ref, used_ref, low_ref, mine_ref, other_ref, cos_ref, sin_ref, key_hbm, value_hbm,
    keep_ref, give_ref, rows_ref, query_ref, fresh_ref, out_ref, key_ref, value_ref, sems,
):
    copies = []
    for g in range(4):
        hbm, ref = ((key_hbm, key_ref), (value_hbm, value_ref))[g // 2]
        part = pl.ds((g % 2) * 16, 16)
        copies.append(pltpu.make_async_copy(hbm.at[part], ref.at[part], sems.at[g]))
        copies[-1].start()
    parity = parity_ref[0]
    for i in range(32):
        rows_ref[i : i + 1, :] = low_ref[plan_ref[2 * i + parity]]
    heads, key, value = project(
        parity, mine_ref[...], other_ref[...], rows_ref[...], cos_ref[...], sin_ref[...]
    )
    for h in range(8):
        query_ref[pl.ds(h, 32, 8), :] = heads[h]
        fresh_ref[pl.ds(h, 32, 8), :] = value
    scale = 1.0 / math.sqrt(HEAD)
    lane = lax.broadcasted_iota(jnp.int32, (128, 128), 1) >> 3
    near_key = key.astype(BF16)
    halves = []
    for half in range(2):
        queries = query_ref[half * 128 : (half + 1) * 128, :].T
        spread = jnp.concatenate(
            [jnp.where(lane == s, queries, 0.0).astype(BF16) for s in range(16)], axis=0
        )
        near = jnp.concatenate(
            [near_key[half * 16 + s : half * 16 + s + 1, :] for s in range(16)], axis=1
        )
        own = dot(jnp.broadcast_to(near, (16, 2048)), spread)[0:1] * scale
        copies[half].wait()
        block = jnp.concatenate([key_ref[half * 16 + s] for s in range(16)], axis=1)
        scores = dot(block, spread) * scale
        valid = lax.broadcasted_iota(jnp.int32, (512, 128), 0) < used_ref[half : half + 1, :]
        top = jnp.max(jnp.where(valid, scores, -jnp.inf), axis=0, keepdims=True)
        top = jnp.maximum(top, own)
        weights = jnp.where(valid, jnp.exp(scores - top), 0.0)
        own_weight = jnp.exp(own - top)
        total = jnp.sum(weights, axis=0, keepdims=True) + own_weight
        pair = jnp.concatenate([own_weight, total, jnp.zeros((6, 128), F32)], axis=0).T
        halves.append((weights.T.astype(BF16), pair))
    for half in range(2):
        copies[2 + half].wait()
        weights, pair = halves[half]
        rows = slice(half * 128, (half + 1) * 128)
        own = pair[:, 0:1].astype(BF16).astype(F32) * fresh_ref[rows, :]
        total = pair[:, 1:2]
        for s in range(16):
            eight = slice(s * 8, (s + 1) * 8)
            out = dot(weights[eight], value_ref[half * 16 + s])
            out_ref[half * 128 + s * 8 : half * 128 + s * 8 + 8, :] = (out + own[eight]) / total[eight]
    outs = [out_ref[pl.ds(h, 32, 8), :] for h in range(8)]
    keep, give = split(parity, outs, key, value)
    keep_ref[...] = keep.astype(BF16)
    give_ref[...] = give.astype(BF16)


def attend_all(plan, parity, used, low, mine, other, cos, sin, keys, values):
    return pl.pallas_call(
        attend_kernel,
        out_shape=[jax.ShapeDtypeStruct((32, 640), BF16)] * 2,
        in_specs=[SMEM] * 2 + [VMEM] * 6 + [ANY] * 2,
        out_specs=[VMEM] * 2,
        scratch_shapes=[
            pltpu.VMEM((32, 1280), F32),
            pltpu.VMEM((256, 128), F32),
            pltpu.VMEM((256, 128), F32),
            pltpu.VMEM((256, 128), F32),
            pltpu.VMEM(keys.shape, BF16),
            pltpu.VMEM(values.shape, BF16),
            pltpu.SemaphoreType.DMA((4,)),
        ],
        cost_estimate=pl.CostEstimate(flops=70_000_000, bytes_accessed=1_000_000, transcendentals=131_072),
        compiler_params=pltpu.CompilerParams(vmem_limit_bytes=20 * 2**20),
        name="attend_all",
    )(plan, parity, used, low, mine, other, cos, sin, keys, values)


def amend_kernel(
    plan_ref, parity_ref, used_ref, row_ref, mine_ref, other_ref, cos_ref, sin_ref, key_ref, value_ref,
    keep_in, give_in, keep_ref, give_ref, query_ref,
):
    parity = parity_ref[0]
    first, last = plan_ref[64], plan_ref[65]
    here = ((first & 1) == parity) & ((last & 1) == parity)
    i = last >> 1
    one = pl.ds(i, 1)
    heads, key, value = project(
        parity, mine_ref[one, :], other_ref[one, :], row_ref[0:1, :], cos_ref[one, :], sin_ref[one, :]
    )
    for h in range(8):
        query_ref[h : h + 1, :] = heads[h]
    out = attend(query_ref[...], key, value, key_ref[...], value_ref[...], used_ref[last])
    keep, give = split(parity, [out[h : h + 1] for h in range(8)], key, value)
    hit = (lax.broadcasted_iota(jnp.int32, (32, 640), 0) == i) & here
    keep_ref[...] = jnp.where(hit, keep, keep_in[...].astype(F32)).astype(BF16)
    give_ref[...] = jnp.where(hit, give, give_in[...].astype(F32)).astype(BF16)


def amend(plan, parity, used, row, mine, other, cos, sin, keys, values, keep, give):
    return pl.pallas_call(
        amend_kernel,
        out_shape=[jax.ShapeDtypeStruct((32, 640), BF16)] * 2,
        in_specs=[SMEM] * 3 + [VMEM] * 9,
        out_specs=[VMEM] * 2,
        scratch_shapes=[pltpu.VMEM((8, 128), F32)],
        cost_estimate=pl.CostEstimate(flops=2_000_000, bytes_accessed=500_000, transcendentals=4096),
        compiler_params=pltpu.CompilerParams(vmem_limit_bytes=4 * 2**20),
        name="amend",
    )(plan, parity, used, row, mine, other, cos, sin, keys, values, keep, give)


def pick_kernel(plan_ref, low_ref, row_ref):
    row_ref[...] = low_ref[plan_ref[plan_ref[64]]]


def pick(plan, low):
    return pl.pallas_call(
        pick_kernel,
        out_shape=jax.ShapeDtypeStruct((1, 1280), F32),
        in_specs=[SMEM, VMEM],
        out_specs=VMEM,
        compiler_params=pltpu.CompilerParams(vmem_limit_bytes=2 * 2**20),
        name="pick",
    )(plan, low)


def weave_kernel(parity_ref, keep_ref, back_ref, out_ref, key_ref, value_ref, rows_ref):
    even, odd = sides(parity_ref[0], keep_ref[...].astype(F32), back_ref[...].astype(F32))
    for c in range(5):
        cols = slice(c * 128, (c + 1) * 128)
        rows_ref[pl.ds(0, 32, 2), :] = even[:, cols]
        rows_ref[pl.ds(1, 32, 2), :] = odd[:, cols]
        both = rows_ref[...].astype(BF16)
        if c < 4:
            out_ref[:, cols] = both
        else:
            key_ref[...] = both[:, 0:64]
            value_ref[...] = both[:, 64:128]


def weave(parity, keep, back):
    return pl.pallas_call(
        weave_kernel,
        out_shape=[
            jax.ShapeDtypeStruct((64, 512), BF16),
            jax.ShapeDtypeStruct((64, 64), BF16),
            jax.ShapeDtypeStruct((64, 64), BF16),
        ],
        in_specs=[SMEM, VMEM, VMEM],
        out_specs=[VMEM] * 3,
        scratch_shapes=[pltpu.VMEM((64, 128), F32)],
        compiler_params=pltpu.CompilerParams(vmem_limit_bytes=2 * 2**20),
        name="weave",
    )(parity, keep, back)


def local(
    hidden, wq, wk, wv, down_maps, up_maps, key_cache, value_cache, filled, positions, requests, slots
):
    t = lax.axis_index("tensor")
    parity = t & 1
    z, y = t & 3, t >> 2
    swap = [(i, i ^ 1) for i in range(16)]

    def z_turn(k):
        return [(4 * a + b, 4 * a + (b + k) % 4) for a in range(4) for b in range(4)]

    def y_turn(k):
        return [(4 * a + b, 4 * ((a + k) % 4) + b) for a in range(4) for b in range(4)]

    sent, plan = prepare(requests, slots, hidden)
    rows = jnp.swapaxes(hidden.reshape(32, 2, 512), 0, 1).reshape(64, 512)
    around_z = [rows] + [lax.ppermute(rows, "tensor", z_turn(k)) for k in (1, 2, 3)]
    recv = lax.all_to_all(sent, ROUTE, 0, 0, tiled=True)
    band = jnp.stack(around_z)
    bands = [band] + [lax.ppermute(band, "tensor", y_turn(k)) for k in (1, 2, 3)]

    low_sent = owner_low(
        recv, down_maps.reshape(96, 8192), up_maps.reshape(32, 10240)
    )
    low_sent, *bands = lax.optimization_barrier((low_sent, *bands))
    low = lax.all_to_all(low_sent, ROUTE, 0, 0, tiled=True)

    turns = jnp.arange(16)
    order = 4 * ((y - (turns >> 2)) & 3) + ((z - turns) & 3)
    order = jnp.concatenate([order, parity[None]]).astype(jnp.int32)
    mine, give, key2, value2 = base_project(
        order, plan, bands, wq, wk.T, wv.T, key_cache[0], value_cache[0], low_sent
    )
    other = lax.ppermute(give, "tensor", swap)

    pos = lax.dynamic_index_in_dim(positions.reshape(32, 2), parity, 1, keepdims=False)
    freq = THETA ** (-2.0 * jnp.arange(64, dtype=F32) / HEAD)
    angle = pos.astype(F32)[:, None] * freq[None, :]
    cos, sin = jnp.cos(angle), jnp.sin(angle)
    cos, sin = jnp.concatenate([cos, cos], 1), jnp.concatenate([-sin, sin], 1)

    which = parity.reshape(1)
    row = lax.ppermute(pick(plan, low), "tensor", swap)
    keys, values = in_hbm(key_cache[0], value_cache[0])
    used = lax.dynamic_index_in_dim(filled.reshape(32, 2), parity, 1, keepdims=False)
    used = jnp.repeat(used, 8).reshape(2, 128)
    keep, give = attend_all(plan, which, used, low, mine, other, cos, sin, keys, values)
    keep, give = amend(
        plan, which, filled, row, mine, other, cos, sin, key2, value2, keep, give
    )
    back = lax.ppermute(give, "tensor", swap)
    return tuple(weave(which, keep, back))


def solution(mesh):
    return jax.shard_map(
        local,
        mesh=mesh,
        in_specs=(
            P("dp", "tensor"),
            P(None, "tensor"),
            P(None, "tensor"),
            P(None, "tensor"),
            P(("dp", "tensor"), None, None),
            P(("dp", "tensor"), None, None),
            P("tensor", "dp", None, None),
            P("tensor", "dp", None, None),
            P("dp"),
            P("dp"),
            P("dp", None),
            P("dp"),
        ),
        out_specs=(P("dp", "tensor"), P("dp", "tensor"), P("dp", "tensor")),
        check_vma=False,
    )
```

```python
import functools
import math

import jax
import jax.numpy as jnp
from jax import lax
from jax.experimental import pallas as pl
from jax.experimental.pallas import tpu as pltpu
from jax.sharding import PartitionSpec as P

HEAD = 128
RANK = 8
THETA = 500000.0
ROUTE = ("tensor", "dp")
BF16 = jnp.bfloat16
F32 = jnp.float32
SMEM = pl.BlockSpec(memory_space=pltpu.SMEM)
VMEM = pl.BlockSpec(memory_space=pltpu.VMEM)
ANY = pl.BlockSpec(memory_space=pl.ANY)
NT = (((1,), (1,)), ((), ()))
dot = functools.partial(jnp.dot, preferred_element_type=F32)
dot_nt = functools.partial(lax.dot_general, dimension_numbers=NT, preferred_element_type=F32)


def prepare_kernel(
    requests_hbm, slots_hbm, hidden_hbm, down_hbm, up_hbm, sent_ref, plan_ref, down_ref, up_ref, hidden_ref,
    rows_ref, wide_ref, requests_ref, slots_ref, sems,
):
    copies = [
        pltpu.make_async_copy(requests_hbm, requests_ref, sems.at[0]),
        pltpu.make_async_copy(slots_hbm, slots_ref, sems.at[1]),
        pltpu.make_async_copy(hidden_hbm, hidden_ref, sems.at[2]),
    ]
    maps = [
        pltpu.make_async_copy(down_hbm, down_ref, sems.at[3]),
        pltpu.make_async_copy(up_hbm, up_ref, sems.at[4]),
    ]
    for copy in copies + maps:
        copy.start()
    rows_ref[...] = jnp.zeros_like(rows_ref)
    for copy in copies:
        copy.wait()
    wide_ref[:, 0:512] = hidden_ref[...].astype(F32)
    first = jnp.int32(-1)
    last = jnp.int32(-1)
    for s in range(64):
        slot = slots_ref[s]
        adapter = requests_ref[0, slot]
        owner = adapter >> 2
        place = (owner & 15) * 8 + (owner >> 4)
        plan_ref[s] = place
        zero = slot == 0
        rank = jnp.where(zero & (first >= 0), 1, 0)
        last = jnp.where(zero, s, last)
        first = jnp.where(zero & (first < 0), s, first)
        code = ((adapter & 3) + 4 * (s % 2)).astype(F32)
        wide_ref[s : s + 1, 512:640] = jnp.full((1, 128), code, F32)
        rows_ref[place, pl.ds(rank, 1), :] = wide_ref[s : s + 1, :]
    plan_ref[64] = first
    plan_ref[65] = last
    sent_ref[...] = rows_ref[...].astype(BF16)
    for copy in maps:
        copy.wait()


def in_hbm(*arrays):
    return [pltpu.with_memory_space_constraint(x, pltpu.HBM) for x in arrays]


def prepare(requests, slots, hidden, down, up):
    return pl.pallas_call(
        prepare_kernel,
        out_shape=[
            pltpu.HBM((128, 2, 640), BF16),
            jax.ShapeDtypeStruct((66,), jnp.int32),
            pltpu.VMEM(down.shape, BF16),
            pltpu.VMEM(up.shape, BF16),
            pltpu.VMEM(hidden.shape, BF16),
        ],
        in_specs=[ANY] * 5,
        out_specs=[VMEM, SMEM, ANY, ANY, VMEM],
        scratch_shapes=[
            pltpu.VMEM((128, 2, 640), F32),
            pltpu.VMEM((64, 640), F32),
            pltpu.SMEM((1, 63), jnp.int32),
            pltpu.SMEM((64,), jnp.int32),
            pltpu.SemaphoreType.DMA((5,)),
        ],
        cost_estimate=pl.CostEstimate(flops=1_000_000, bytes_accessed=500_000, transcendentals=0),
        compiler_params=pltpu.CompilerParams(vmem_limit_bytes=4 * 2**20),
        name="prepare",
    )(*in_hbm(requests, slots, hidden, down, up))


def band_kernel(_, h0_ref, h1_ref, h2_ref, h3_ref, out_ref):
    for k, ref in enumerate((h0_ref, h1_ref, h2_ref, h3_ref)):
        out_ref[k] = ref[...]


def stack_band(plan, blocks):
    return pl.pallas_call(
        band_kernel,
        out_shape=jax.ShapeDtypeStruct((4, 64, 512), BF16),
        in_specs=[SMEM] + [VMEM] * 4,
        out_specs=VMEM,
        cost_estimate=pl.CostEstimate(flops=1000, bytes_accessed=500_000, transcendentals=0),
        compiler_params=pltpu.CompilerParams(vmem_limit_bytes=4 * 2**20),
        name="stack_band",
    )(plan, *blocks)


def owner_kernel(recv_ref, down_ref, up_ref, out_ref, coords_ref, code_ref):
    acc = jnp.zeros((16, 96), F32)
    for t in range(16):
        acc = acc + dot_nt(
            recv_ref[t * 8 : (t + 1) * 8, :, 0:512].reshape(16, 512),
            down_ref[:, t * 512 : (t + 1) * 512],
        )
    coords_ref[:, 0:96] = acc.astype(BF16).astype(F32)
    code_ref[...] = recv_ref[0:8, :, 512:640].reshape(16, 128).astype(F32)
    one, two = coords_ref[pl.ds(0, 8, 2), :], coords_ref[pl.ds(1, 8, 2), :]
    code = code_ref[pl.ds(0, 8, 2), :][:, 0:1].astype(jnp.int32)
    odd = code >= 4
    coords = jnp.concatenate([jnp.where(odd, two, one), jnp.where(odd, one, two)], axis=0)
    ids = jnp.concatenate([code, code], axis=0) & 3
    mine = (lax.broadcasted_iota(jnp.int32, (16, 32), 1) >> 3) == ids
    blocks = []
    for b in range(3):
        block = jnp.concatenate(
            [coords[:, a * 24 + b * 8 : a * 24 + b * 8 + 8] for a in range(4)], axis=1
        )
        blocks.append(jnp.where(mine, block, 0.0).astype(BF16))
    low_key = dot(blocks[1], up_ref[:, 8192:9216])
    low_value = dot(blocks[2], up_ref[:, 9216:10240])
    for j in range(8):
        low_query = dot(blocks[0], up_ref[:, j * 1024 : (j + 1) * 1024])
        head = slice(j * 128, (j + 1) * 128)
        for p in range(2):
            rows, half = slice((2 * j + p) * 8, (2 * j + p + 1) * 8), slice(p * 8, p * 8 + 8)
            out_ref[rows, 0, 0:1024] = low_query[half]
            out_ref[rows, 0, 1024:1152] = low_key[half, head]
            out_ref[rows, 0, 1152:1280] = low_value[half, head]


def owner_low(recv, down, up):
    return pl.pallas_call(
        owner_kernel,
        out_shape=jax.ShapeDtypeStruct((128, 1, 1280), F32),
        in_specs=[VMEM] * 3,
        out_specs=VMEM,
        scratch_shapes=[
            pltpu.VMEM((16, 128), F32),
            pltpu.VMEM((16, 128), F32),
        ],
        cost_estimate=pl.CostEstimate(flops=40_000_000, bytes_accessed=3_400_000, transcendentals=0),
        compiler_params=pltpu.CompilerParams(vmem_limit_bytes=8 * 2**20),
        name="owner_low",
    )(recv, down, up)


def weight_copies(rows, wq_hbm, wk_hbm, wv_hbm, wq_ref, wkv_ref, sems):
    copies = []
    for i, row in enumerate(rows):
        part = pl.ds(pl.multiple_of(row, 512), 512)
        copies.append(
            [
                pltpu.make_async_copy(wk_hbm.at[:, part], wkv_ref.at[i, 0:64], sems.at[0, i]),
                pltpu.make_async_copy(wv_hbm.at[:, part], wkv_ref.at[i, 64:128], sems.at[1, i]),
                pltpu.make_async_copy(wq_hbm.at[part], wq_ref.at[i], sems.at[2, i]),
            ]
        )
    for block in copies:
        for copy in block:
            copy.start()
    return copies


def add_blocks(hiddens, copies, wq_ref, wkv_ref, q, kv):
    for i, hidden in enumerate(hiddens):
        for copy in copies[i]:
            copy.wait()
        q = q + dot(hidden, wq_ref[i])
        kv = kv + dot_nt(hidden, wkv_ref[i])
    return q, kv


def base_kernel(
    place_ref, h0_ref, h1_ref, h3_ref, wq_hbm, wk_hbm, wv_hbm, _, out_ref, wq_ref, wkv_ref, sems
):
    y, z = place_ref[0], place_ref[1]
    rows = [(((y - a) & 3) * 4 + ((z - b) & 3)) * 512 for a in (0, 1, 3) for b in range(4)]
    copies = weight_copies(rows, wq_hbm, wk_hbm, wv_hbm, wq_ref, wkv_ref, sems)
    hiddens = [ref[b] for ref in (h0_ref, h1_ref, h3_ref) for b in range(4)]
    q, kv = add_blocks(
        hiddens, copies, wq_ref, wkv_ref, jnp.zeros((64, 512), F32), jnp.zeros((64, 128), F32)
    )
    out_ref[:, 0:512] = q
    out_ref[:, 512:640] = kv


def rest_kernel(
    place_ref, plan_ref, part_ref, ha_ref, hb_ref, wq_hbm, wk_hbm, wv_hbm, key_hbm, value_hbm,
    mine_ref, give_ref, key2_ref, value2_ref, wq_ref, wkv_ref, acc_ref, sems, cache_sems,
):
    y, z = place_ref[0], place_ref[1]
    rows = [(((y - 2) & 3) * 4 + ((z - b) & 3)) * 512 for b in range(4)]
    copies = weight_copies(rows, wq_hbm, wk_hbm, wv_hbm, wq_ref, wkv_ref, sems)
    cache = [
        pltpu.make_async_copy(key_hbm.at[plan_ref[65] >> 1], key2_ref, cache_sems.at[0]),
        pltpu.make_async_copy(value_hbm.at[plan_ref[65] >> 1], value2_ref, cache_sems.at[1]),
    ]
    for copy in cache:
        copy.start()
    hiddens = [ha_ref[0], ha_ref[1], hb_ref[0], hb_ref[1]]
    q, kv = add_blocks(hiddens, copies, wq_ref, wkv_ref, part_ref[:, 0:512], part_ref[:, 512:640])
    parity = z & 1
    for c in range(5):
        cols = slice(c * 128, (c + 1) * 128)
        acc_ref[...] = q[:, cols] if c < 4 else kv
        even, odd = acc_ref[pl.ds(0, 32, 2), :], acc_ref[pl.ds(1, 32, 2), :]
        mine_ref[:, cols], give_ref[:, cols] = sides(parity, even, odd)
    for copy in cache:
        copy.wait()


def base_project(place, bands, wq, wkt, wvt, after):
    return pl.pallas_call(
        base_kernel,
        out_shape=jax.ShapeDtypeStruct((64, 640), F32),
        in_specs=[SMEM] + [VMEM] * 3 + [ANY] * 4,
        out_specs=VMEM,
        scratch_shapes=[
            pltpu.VMEM((12, 512, 512), BF16),
            pltpu.VMEM((12, 128, 512), BF16),
            pltpu.SemaphoreType.DMA((3, 12)),
        ],
        cost_estimate=pl.CostEstimate(flops=503_000_000, bytes_accessed=8_800_000, transcendentals=0),
        compiler_params=pltpu.CompilerParams(vmem_limit_bytes=16 * 2**20),
        name="base_project",
    )(place, *bands, *in_hbm(wq, wkt, wvt), after)


def base_rest(place, plan, part, halves, wq, wkt, wvt, keys, values):
    return pl.pallas_call(
        rest_kernel,
        out_shape=[
            jax.ShapeDtypeStruct((32, 640), F32),
            jax.ShapeDtypeStruct((32, 640), F32),
            jax.ShapeDtypeStruct(keys.shape[1:], BF16),
            jax.ShapeDtypeStruct(values.shape[1:], BF16),
        ],
        in_specs=[SMEM] * 2 + [VMEM] * 3 + [ANY] * 5,
        out_specs=[VMEM] * 4,
        scratch_shapes=[
            pltpu.VMEM((4, 512, 512), BF16),
            pltpu.VMEM((4, 128, 512), BF16),
            pltpu.VMEM((64, 128), F32),
            pltpu.SemaphoreType.DMA((3, 4)),
            pltpu.SemaphoreType.DMA((2,)),
        ],
        cost_estimate=pl.CostEstimate(flops=168_000_000, bytes_accessed=3_200_000, transcendentals=0),
        compiler_params=pltpu.CompilerParams(vmem_limit_bytes=8 * 2**20),
        name="base_rest",
    )(place, plan, part, *halves, *in_hbm(wq, wkt, wvt, keys, values))


def rotate(part, cos, sin):
    return part * cos + pltpu.roll(part, 64, 1) * sin


def attend(query, key_new, value_new, keys, values, used):
    scale = 1.0 / math.sqrt(HEAD)
    scores = dot_nt(query.astype(BF16), keys) * scale
    own = jnp.sum(query * key_new, axis=1, keepdims=True) * scale
    valid = lax.broadcasted_iota(jnp.int32, scores.shape, 1) < used
    top = jnp.max(jnp.where(valid, scores, -jnp.inf), axis=1, keepdims=True)
    top = jnp.maximum(top, own)
    weights = jnp.where(valid, jnp.exp(scores - top), 0.0)
    own_weight = jnp.exp(own - top)
    total = jnp.sum(weights, axis=1, keepdims=True) + own_weight
    out = dot(weights.astype(BF16), values) + own_weight.astype(BF16).astype(F32) * value_new
    return out / total


def sides(parity, mine, other):
    even = parity == 0
    return jnp.where(even, mine, other), jnp.where(even, other, mine)


def project(parity, mine, other, low, cos, sin):
    def rounded(x):
        return x.astype(BF16).astype(F32)

    left, right = sides(parity, mine, other)
    heads = []
    for h in range(8):
        base = (left if h < 4 else right)[:, (h % 4) * 128 : (h % 4 + 1) * 128]
        heads.append(rounded(rotate(base + low[:, h * 128 : (h + 1) * 128], cos, sin)))
    key = jnp.concatenate([left[:, 512:576], right[:, 512:576]], axis=1) + low[:, 1024:1152]
    value = jnp.concatenate([left[:, 576:640], right[:, 576:640]], axis=1) + low[:, 1152:1280]
    return heads, rounded(rotate(key, cos, sin)), rounded(value)


def split(parity, outs, key, value):
    low = jnp.concatenate(outs[:4] + [key[:, :64], value[:, :64]], axis=1)
    high = jnp.concatenate(outs[4:] + [key[:, 64:], value[:, 64:]], axis=1)
    return sides(parity, low, high)


def attend_kernel(
    plan_ref, parity_ref, used_ref, low_ref, mine_ref, other_ref, cos_ref, sin_ref, key_hbm, value_hbm,
    keep_ref, give_ref, rows_ref, query_ref, near_ref, fresh_ref, out_ref, key_ref, value_ref, sems,
):
    copies = []
    for g in range(4):
        hbm, ref = ((key_hbm, key_ref), (value_hbm, value_ref))[g // 2]
        part = pl.ds((g % 2) * 16, 16)
        copies.append(pltpu.make_async_copy(hbm.at[part], ref.at[part], sems.at[g]))
        copies[-1].start()
    parity = parity_ref[0]
    for i in range(32):
        rows_ref[i : i + 1, :] = low_ref[plan_ref[2 * i + parity]]
    heads, key, value = project(
        parity, mine_ref[...], other_ref[...], rows_ref[...], cos_ref[...], sin_ref[...]
    )
    for h in range(8):
        query_ref[pl.ds(h, 32, 8), :] = heads[h]
        near_ref[pl.ds(h, 32, 8), :] = key
        fresh_ref[pl.ds(h, 32, 8), :] = value
    scale = 1.0 / math.sqrt(HEAD)
    halves = []
    for half in range(2):
        rows = slice(half * 128, (half + 1) * 128)
        query = query_ref[rows, :]
        own = jnp.sum(query * near_ref[rows, :], axis=1, keepdims=True) * scale
        copies[half].wait()
        scores = jnp.concatenate(
            [dot_nt(query[s * 8 : s * 8 + 8].astype(BF16), key_ref[half * 16 + s]) for s in range(16)], axis=0
        ) * scale
        valid = lax.broadcasted_iota(jnp.int32, (128, 512), 1) < used_ref[rows, :]
        top = jnp.max(jnp.where(valid, scores, -jnp.inf), axis=1, keepdims=True)
        top = jnp.maximum(top, own)
        weights = jnp.where(valid, jnp.exp(scores - top), 0.0)
        own_weight = jnp.exp(own - top)
        total = jnp.sum(weights, axis=1, keepdims=True) + own_weight
        halves.append((weights.astype(BF16), own_weight, total))
    for half in range(2):
        copies[2 + half].wait()
        weights, own_weight, total = halves[half]
        rows = slice(half * 128, (half + 1) * 128)
        own = own_weight.astype(BF16).astype(F32) * fresh_ref[rows, :]
        out = jnp.concatenate(
            [dot(weights[s * 8 : s * 8 + 8], value_ref[half * 16 + s]) for s in range(16)], axis=0
        )
        out_ref[rows, :] = (out + own) / total
    outs = [out_ref[pl.ds(h, 32, 8), :] for h in range(8)]
    keep, give = split(parity, outs, key, value)
    keep_ref[...] = keep.astype(BF16)
    give_ref[...] = give.astype(BF16)


def attend_all(plan, parity, used, low, mine, other, cos, sin, keys, values):
    return pl.pallas_call(
        attend_kernel,
        out_shape=[jax.ShapeDtypeStruct((32, 640), BF16)] * 2,
        in_specs=[SMEM] * 2 + [VMEM] * 6 + [ANY] * 2,
        out_specs=[VMEM] * 2,
        scratch_shapes=[
            pltpu.VMEM((32, 1280), F32),
            pltpu.VMEM((256, 128), F32),
            pltpu.VMEM((256, 128), F32),
            pltpu.VMEM((256, 128), F32),
            pltpu.VMEM((256, 128), F32),
            pltpu.VMEM(keys.shape, BF16),
            pltpu.VMEM(values.shape, BF16),
            pltpu.SemaphoreType.DMA((4,)),
        ],
        cost_estimate=pl.CostEstimate(flops=70_000_000, bytes_accessed=1_000_000, transcendentals=131_072),
        compiler_params=pltpu.CompilerParams(vmem_limit_bytes=20 * 2**20),
        name="attend_all",
    )(plan, parity, used, low, mine, other, cos, sin, keys, values)


def amend_kernel(
    plan_ref, parity_ref, used_ref, row_ref, mine_ref, other_ref, cos_ref, sin_ref, key_ref, value_ref,
    keep_in, give_in, keep_ref, give_ref, query_ref,
):
    parity = parity_ref[0]
    first, last = plan_ref[64], plan_ref[65]
    here = ((first & 1) == parity) & ((last & 1) == parity)
    i = last >> 1
    one = pl.ds(i, 1)
    heads, key, value = project(
        parity, mine_ref[one, :], other_ref[one, :], row_ref[0:1, :], cos_ref[one, :], sin_ref[one, :]
    )
    for h in range(8):
        query_ref[h : h + 1, :] = heads[h]
    out = attend(query_ref[...], key, value, key_ref[...], value_ref[...], used_ref[last])
    keep, give = split(parity, [out[h : h + 1] for h in range(8)], key, value)
    hit = (lax.broadcasted_iota(jnp.int32, (32, 640), 0) == i) & here
    keep_ref[...] = jnp.where(hit, keep, keep_in[...].astype(F32)).astype(BF16)
    give_ref[...] = jnp.where(hit, give, give_in[...].astype(F32)).astype(BF16)


def amend(plan, parity, used, row, mine, other, cos, sin, keys, values, keep, give):
    return pl.pallas_call(
        amend_kernel,
        out_shape=[jax.ShapeDtypeStruct((32, 640), BF16)] * 2,
        in_specs=[SMEM] * 3 + [VMEM] * 9,
        out_specs=[VMEM] * 2,
        scratch_shapes=[pltpu.VMEM((8, 128), F32)],
        cost_estimate=pl.CostEstimate(flops=2_000_000, bytes_accessed=500_000, transcendentals=4096),
        compiler_params=pltpu.CompilerParams(vmem_limit_bytes=4 * 2**20),
        name="amend",
    )(plan, parity, used, row, mine, other, cos, sin, keys, values, keep, give)


def pick_kernel(plan_ref, low_ref, row_ref):
    row_ref[...] = low_ref[plan_ref[plan_ref[64]]]


def pick(plan, low):
    return pl.pallas_call(
        pick_kernel,
        out_shape=jax.ShapeDtypeStruct((1, 1280), F32),
        in_specs=[SMEM, VMEM],
        out_specs=VMEM,
        compiler_params=pltpu.CompilerParams(vmem_limit_bytes=2 * 2**20),
        name="pick",
    )(plan, low)


def weave_kernel(parity_ref, keep_ref, back_ref, out_ref, key_ref, value_ref, rows_ref):
    even, odd = sides(parity_ref[0], keep_ref[...].astype(F32), back_ref[...].astype(F32))
    for c in range(5):
        cols = slice(c * 128, (c + 1) * 128)
        rows_ref[pl.ds(0, 32, 2), :] = even[:, cols]
        rows_ref[pl.ds(1, 32, 2), :] = odd[:, cols]
        both = rows_ref[...].astype(BF16)
        if c < 4:
            out_ref[:, cols] = both
        else:
            key_ref[...] = both[:, 0:64]
            value_ref[...] = both[:, 64:128]


def weave(parity, keep, back):
    return pl.pallas_call(
        weave_kernel,
        out_shape=[
            jax.ShapeDtypeStruct((64, 512), BF16),
            jax.ShapeDtypeStruct((64, 64), BF16),
            jax.ShapeDtypeStruct((64, 64), BF16),
        ],
        in_specs=[SMEM, VMEM, VMEM],
        out_specs=[VMEM] * 3,
        scratch_shapes=[pltpu.VMEM((64, 128), F32)],
        compiler_params=pltpu.CompilerParams(vmem_limit_bytes=2 * 2**20),
        name="weave",
    )(parity, keep, back)


def local(
    hidden, wq, wk, wv, down_maps, up_maps, key_cache, value_cache, filled, positions, requests, slots
):
    t = lax.axis_index("tensor")
    parity = t & 1
    z, y = t & 3, t >> 2
    swap = [(i, i ^ 1) for i in range(16)]

    def z_turn(k):
        return [(4 * a + b, 4 * a + (b + k) % 4) for a in range(4) for b in range(4)]

    def y_turn(k):
        return [(4 * a + b, 4 * ((a + k) % 4) + b) for a in range(4) for b in range(4)]

    sent, plan, down_near, up_near, hidden_near = prepare(
        requests, slots, hidden, down_maps.reshape(96, 8192), up_maps.reshape(32, 10240)
    )
    around_z = [hidden] + [lax.ppermute(hidden, "tensor", z_turn(k)) for k in (1, 2, 3)]
    recv = lax.all_to_all(sent, ROUTE, 0, 0, tiled=True)
    band = stack_band(plan, [hidden_near] + around_z[1:])
    up, down = (lax.ppermute(band, "tensor", y_turn(k)) for k in (1, 3))

    halves = [
        lax.ppermute(up[0:2], "tensor", y_turn(1)), lax.ppermute(down[2:4], "tensor", y_turn(3))
    ]
    recv, up, down = lax.optimization_barrier((recv, up, down))
    low_sent = owner_low(recv, down_near, up_near)
    low_sent, *halves = lax.optimization_barrier((low_sent, *halves))
    low = lax.all_to_all(low_sent, ROUTE, 0, 0, tiled=True)

    place = jnp.stack([y, z]).astype(jnp.int32)
    part = base_project(place, (band, up, down), wq, wk.T, wv.T, low_sent)
    mine, give, key2, value2 = base_rest(
        place, plan, part, halves, wq, wk.T, wv.T, key_cache[0], value_cache[0]
    )
    other = lax.ppermute(give, "tensor", swap)

    pos = lax.dynamic_index_in_dim(positions.reshape(32, 2), parity, 1, keepdims=False)
    freq = THETA ** (-2.0 * jnp.arange(64, dtype=F32) / HEAD)
    angle = pos.astype(F32)[:, None] * freq[None, :]
    cos, sin = jnp.cos(angle), jnp.sin(angle)
    cos, sin = jnp.concatenate([cos, cos], 1), jnp.concatenate([-sin, sin], 1)

    which = parity.reshape(1)
    row = lax.ppermute(pick(plan, low), "tensor", swap)
    keys, values = in_hbm(key_cache[0], value_cache[0])
    used = lax.dynamic_index_in_dim(filled.reshape(32, 2), parity, 1, keepdims=False)
    used = jnp.repeat(used, 8).reshape(256, 1)
    keep, give = attend_all(plan, which, used, low, mine, other, cos, sin, keys, values)
    keep, give = amend(
        plan, which, filled, row, mine, other, cos, sin, key2, value2, keep, give
    )
    back = lax.ppermute(give, "tensor", swap)
    return tuple(weave(which, keep, back))


def solution(mesh):
    return jax.shard_map(
        local,
        mesh=mesh,
        in_specs=(
            P("dp", "tensor"),
            P(None, "tensor"),
            P(None, "tensor"),
            P(None, "tensor"),
            P(("dp", "tensor"), None, None),
            P(("dp", "tensor"), None, None),
            P("tensor", "dp", None, None),
            P("tensor", "dp", None, None),
            P("dp"),
            P("dp"),
            P("dp", None),
            P("dp"),
        ),
        out_specs=(P("dp", "tensor"), P("dp", "tensor"), P("dp", "tensor")),
        check_vma=False,
    )
```

```python
import functools
import math

import jax
import jax.numpy as jnp
from jax import lax
from jax.experimental import pallas as pl
from jax.experimental.pallas import tpu as pltpu
from jax.sharding import PartitionSpec as P

HEAD = 128
RANK = 8
THETA = 500000.0
ROUTE = ("tensor", "dp")
BF16 = jnp.bfloat16
F32 = jnp.float32
SMEM = pl.BlockSpec(memory_space=pltpu.SMEM)
VMEM = pl.BlockSpec(memory_space=pltpu.VMEM)
ANY = pl.BlockSpec(memory_space=pl.ANY)
NT = (((1,), (1,)), ((), ()))
dot = functools.partial(jnp.dot, preferred_element_type=F32)
dot_nt = functools.partial(lax.dot_general, dimension_numbers=NT, preferred_element_type=F32)


def plan_kernel(
    z_ref, requests_hbm, slots_hbm, hidden_hbm, down_hbm, up_hbm,
    plan_ref, spread_ref, code_ref, down_ref, up_ref, hidden_ref,
    eye_ref, wide_ref, requests_ref, slots_ref, sems,
):
    copies = [
        pltpu.make_async_copy(requests_hbm, requests_ref, sems.at[0]),
        pltpu.make_async_copy(slots_hbm, slots_ref, sems.at[1]),
    ]
    near = [
        pltpu.make_async_copy(hidden_hbm, hidden_ref, sems.at[2]),
        pltpu.make_async_copy(down_hbm, down_ref, sems.at[3]),
        pltpu.make_async_copy(up_hbm, up_ref, sems.at[4]),
    ]
    for copy in copies + near:
        copy.start()
    spread_ref[...] = jnp.zeros_like(spread_ref)
    code_ref[...] = jnp.zeros_like(code_ref)
    shape = eye_ref.shape
    rows, cols = (lax.broadcasted_iota(jnp.int32, shape, d) for d in range(2))
    eye_ref[...] = jnp.where(rows == cols, 1.0, 0.0)
    for copy in copies:
        copy.wait()
    z = z_ref[0]
    first = jnp.int32(-1)
    last = jnp.int32(-1)
    for s in range(64):
        slot = slots_ref[s]
        adapter = requests_ref[0, slot]
        owner = adapter >> 2
        place = (owner & 15) * 8 + (owner >> 4)
        plan_ref[s] = place
        zero = slot == 0
        rank = jnp.where(zero & (first >= 0), 1, 0)
        last = jnp.where(zero, s, last)
        first = jnp.where(zero & (first < 0), s, first)
        code = ((adapter & 3) + 4 * (s % 2)).astype(F32)
        wide_ref[s : s + 1, :] = jnp.full((1, 128), code, F32)
        row = pl.ds(((place >> 5) * 8 + (place & 7)) * 2 + rank, 1)

        @pl.when(((place >> 3) & 3) == z)
        def _():
            spread_ref[row, :] = eye_ref[s : s + 1, :]
            code_ref[row, :] = wide_ref[s : s + 1, :]

    plan_ref[64] = first
    plan_ref[65] = last
    for copy in near:
        copy.wait()


def in_hbm(*arrays):
    return [pltpu.with_memory_space_constraint(x, pltpu.HBM) for x in arrays]


def make_plan(z, requests, slots, hidden, down, up):
    return pl.pallas_call(
        plan_kernel,
        out_shape=[
            jax.ShapeDtypeStruct((66,), jnp.int32),
            jax.ShapeDtypeStruct((64, 128), F32),
            jax.ShapeDtypeStruct((64, 128), F32),
            pltpu.VMEM(down.shape, BF16),
            pltpu.VMEM(up.shape, BF16),
            pltpu.VMEM(hidden.shape, BF16),
        ],
        in_specs=[SMEM] + [ANY] * 5,
        out_specs=[SMEM, VMEM, VMEM, ANY, ANY, VMEM],
        scratch_shapes=[
            pltpu.VMEM((64, 128), F32),
            pltpu.VMEM((64, 128), F32),
            pltpu.SMEM((1, 63), jnp.int32),
            pltpu.SMEM((64,), jnp.int32),
            pltpu.SemaphoreType.DMA((5,)),
        ],
        cost_estimate=pl.CostEstimate(flops=1_000_000, bytes_accessed=500_000, transcendentals=0),
        compiler_params=pltpu.CompilerParams(vmem_limit_bytes=4 * 2**20),
        name="make_plan",
    )(z, *in_hbm(requests, slots, hidden, down, up))


def send_kernel(spread_ref, code_ref, h0_ref, h1_ref, h2_ref, h3_ref, sent_ref):
    spread = spread_ref[:, 0:64].astype(BF16)
    for k, ref in enumerate((h0_ref, h1_ref, h2_ref, h3_ref)):
        rows = dot(spread, ref[...])
        sent_ref[:, :, k * 512 : (k + 1) * 512] = rows.reshape(32, 2, 512).astype(BF16)
    sent_ref[:, :, 2048:2176] = code_ref[...].reshape(32, 2, 128).astype(BF16)


def send_rows(spread, code, blocks):
    return pl.pallas_call(
        send_kernel,
        out_shape=pltpu.HBM((32, 2, 2176), BF16),
        in_specs=[VMEM] * 6,
        out_specs=VMEM,
        cost_estimate=pl.CostEstimate(flops=1_000_000, bytes_accessed=500_000, transcendentals=0),
        compiler_params=pltpu.CompilerParams(vmem_limit_bytes=4 * 2**20),
        name="send_rows",
    )(spread, code, *blocks)


def band_kernel(_, h0_ref, h1_ref, h2_ref, h3_ref, out_ref):
    for k, ref in enumerate((h0_ref, h1_ref, h2_ref, h3_ref)):
        out_ref[k] = ref[...]


def stack_band(plan, blocks):
    return pl.pallas_call(
        band_kernel,
        out_shape=jax.ShapeDtypeStruct((4, 64, 512), BF16),
        in_specs=[SMEM] + [VMEM] * 4,
        out_specs=VMEM,
        cost_estimate=pl.CostEstimate(flops=1000, bytes_accessed=500_000, transcendentals=0),
        compiler_params=pltpu.CompilerParams(vmem_limit_bytes=4 * 2**20),
        name="stack_band",
    )(plan, *blocks)


def halves_kernel(up_ref, down_ref, a_ref, b_ref):
    a_ref[...] = up_ref[0:2]
    b_ref[...] = down_ref[2:4]


def take_halves(up, down):
    return pl.pallas_call(
        halves_kernel,
        out_shape=[jax.ShapeDtypeStruct((2, 64, 512), BF16)] * 2,
        in_specs=[VMEM] * 2,
        out_specs=[VMEM] * 2,
        cost_estimate=pl.CostEstimate(flops=1000, bytes_accessed=500_000, transcendentals=0),
        compiler_params=pltpu.CompilerParams(vmem_limit_bytes=4 * 2**20),
        name="take_halves",
    )(up, down)


def owner_kernel(z_ref, recv_ref, down_ref, up_ref, out_ref, coords_ref, code_ref):
    z = z_ref[0]
    acc = jnp.zeros((16, 96), F32)
    for y in range(4):
        for k in range(4):
            rows = recv_ref[y * 8 : (y + 1) * 8, :, k * 512 : (k + 1) * 512].reshape(16, 512)
            cols = pl.ds(pl.multiple_of((4 * y + ((z - k) & 3)) * 512, 512), 512)
            acc = acc + dot_nt(rows, down_ref[:, cols])
    coords_ref[:, 0:96] = acc.astype(BF16).astype(F32)
    code_ref[...] = recv_ref[0:8, :, 2048:2176].reshape(16, 128).astype(F32)
    one, two = coords_ref[pl.ds(0, 8, 2), :], coords_ref[pl.ds(1, 8, 2), :]
    code = code_ref[pl.ds(0, 8, 2), :][:, 0:1].astype(jnp.int32)
    odd = code >= 4
    coords = jnp.concatenate([jnp.where(odd, two, one), jnp.where(odd, one, two)], axis=0)
    ids = jnp.concatenate([code, code], axis=0) & 3
    mine = (lax.broadcasted_iota(jnp.int32, (16, 32), 1) >> 3) == ids
    blocks = []
    for b in range(3):
        block = jnp.concatenate(
            [coords[:, a * 24 + b * 8 : a * 24 + b * 8 + 8] for a in range(4)], axis=1
        )
        blocks.append(jnp.where(mine, block, 0.0).astype(BF16))
    low_key = dot(blocks[1], up_ref[:, 8192:9216])
    low_value = dot(blocks[2], up_ref[:, 9216:10240])
    for j in range(8):
        low_query = dot(blocks[0], up_ref[:, j * 1024 : (j + 1) * 1024])
        head = slice(j * 128, (j + 1) * 128)
        for p in range(2):
            rows, half = slice((2 * j + p) * 8, (2 * j + p + 1) * 8), slice(p * 8, p * 8 + 8)
            out_ref[rows, 0, 0:1024] = low_query[half]
            out_ref[rows, 0, 1024:1152] = low_key[half, head]
            out_ref[rows, 0, 1152:1280] = low_value[half, head]


def owner_low(z, recv, down, up):
    return pl.pallas_call(
        owner_kernel,
        out_shape=jax.ShapeDtypeStruct((128, 1, 1280), F32),
        in_specs=[SMEM] + [VMEM] * 3,
        out_specs=VMEM,
        scratch_shapes=[
            pltpu.VMEM((16, 128), F32),
            pltpu.VMEM((16, 128), F32),
        ],
        cost_estimate=pl.CostEstimate(flops=40_000_000, bytes_accessed=3_400_000, transcendentals=0),
        compiler_params=pltpu.CompilerParams(vmem_limit_bytes=8 * 2**20),
        name="owner_low",
    )(z, recv, down, up)


def weight_copies(rows, wq_hbm, wk_hbm, wv_hbm, wq_ref, wkv_ref, sems):
    copies = []
    for i, row in enumerate(rows):
        part = pl.ds(pl.multiple_of(row, 512), 512)
        copies.append(
            [
                pltpu.make_async_copy(wk_hbm.at[:, part], wkv_ref.at[i, 0:64], sems.at[0, i]),
                pltpu.make_async_copy(wv_hbm.at[:, part], wkv_ref.at[i, 64:128], sems.at[1, i]),
                pltpu.make_async_copy(wq_hbm.at[part], wq_ref.at[i], sems.at[2, i]),
            ]
        )
    for block in copies:
        for copy in block:
            copy.start()
    return copies


def add_blocks(hiddens, copies, wq_ref, wkv_ref, q, kv):
    for i, hidden in enumerate(hiddens):
        for copy in copies[i]:
            copy.wait()
        q = q + dot(hidden, wq_ref[i])
        kv = kv + dot_nt(hidden, wkv_ref[i])
    return q, kv


def base_kernel(
    place_ref, plan_ref, h0_ref, h1_ref, ha_ref, hb_ref, h3_ref, wq_hbm, wk_hbm, wv_hbm, key_hbm, value_hbm, _,
    mine_ref, give_ref, key2_ref, value2_ref, wq_ref, wkv_ref, acc_ref, sems, cache_sems,
):
    y, z = place_ref[0], place_ref[1]
    rows = [(((y - a) & 3) * 4 + ((z - b) & 3)) * 512 for a in range(4) for b in range(4)]
    copies = weight_copies(rows, wq_hbm, wk_hbm, wv_hbm, wq_ref, wkv_ref, sems)
    cache = [
        pltpu.make_async_copy(key_hbm.at[plan_ref[65] >> 1], key2_ref, cache_sems.at[0]),
        pltpu.make_async_copy(value_hbm.at[plan_ref[65] >> 1], value2_ref, cache_sems.at[1]),
    ]
    for copy in cache:
        copy.start()
    hiddens = [ref[b] for ref in (h0_ref, h1_ref) for b in range(4)]
    hiddens += [ha_ref[0], ha_ref[1], hb_ref[0], hb_ref[1]] + [h3_ref[b] for b in range(4)]
    q, kv = jnp.zeros((64, 512), F32), jnp.zeros((64, 128), F32)
    for i, hidden in enumerate(hiddens):
        for copy in copies[i]:
            copy.wait()
        q = q + dot(hidden, wq_ref[i])
        kv = kv + dot_nt(hidden, wkv_ref[i])
    parity = z & 1
    for c in range(5):
        cols = slice(c * 128, (c + 1) * 128)
        acc_ref[...] = q[:, cols] if c < 4 else kv
        even, odd = acc_ref[pl.ds(0, 32, 2), :], acc_ref[pl.ds(1, 32, 2), :]
        mine_ref[:, cols], give_ref[:, cols] = sides(parity, even, odd)
    for copy in cache:
        copy.wait()


def base_project(place, plan, bands, wq, wkt, wvt, keys, values, after):
    return pl.pallas_call(
        base_kernel,
        out_shape=[
            jax.ShapeDtypeStruct((32, 640), F32),
            jax.ShapeDtypeStruct((32, 640), F32),
            jax.ShapeDtypeStruct(keys.shape[1:], BF16),
            jax.ShapeDtypeStruct(values.shape[1:], BF16),
        ],
        in_specs=[SMEM] * 2 + [VMEM] * 5 + [ANY] * 6,
        out_specs=[VMEM] * 4,
        scratch_shapes=[
            pltpu.VMEM((16, 512, 512), BF16),
            pltpu.VMEM((16, 128, 512), BF16),
            pltpu.VMEM((64, 128), F32),
            pltpu.SemaphoreType.DMA((3, 16)),
            pltpu.SemaphoreType.DMA((2,)),
        ],
        cost_estimate=pl.CostEstimate(flops=671_000_000, bytes_accessed=11_700_000, transcendentals=0),
        compiler_params=pltpu.CompilerParams(vmem_limit_bytes=16 * 2**20),
        name="base_project",
    )(place, plan, *bands, *in_hbm(wq, wkt, wvt, keys, values), after)


def rotate(part, cos, sin):
    return part * cos + pltpu.roll(part, 64, 1) * sin


def attend(query, key_new, value_new, keys, values, used):
    scale = 1.0 / math.sqrt(HEAD)
    scores = dot_nt(query.astype(BF16), keys) * scale
    own = jnp.sum(query * key_new, axis=1, keepdims=True) * scale
    valid = lax.broadcasted_iota(jnp.int32, scores.shape, 1) < used
    top = jnp.max(jnp.where(valid, scores, -jnp.inf), axis=1, keepdims=True)
    top = jnp.maximum(top, own)
    weights = jnp.where(valid, jnp.exp(scores - top), 0.0)
    own_weight = jnp.exp(own - top)
    total = jnp.sum(weights, axis=1, keepdims=True) + own_weight
    out = dot(weights.astype(BF16), values) + own_weight.astype(BF16).astype(F32) * value_new
    return out / total


def sides(parity, mine, other):
    even = parity == 0
    return jnp.where(even, mine, other), jnp.where(even, other, mine)


def project(parity, mine, other, low, cos, sin):
    def rounded(x):
        return x.astype(BF16).astype(F32)

    left, right = sides(parity, mine, other)
    heads = []
    for h in range(8):
        base = (left if h < 4 else right)[:, (h % 4) * 128 : (h % 4 + 1) * 128]
        heads.append(rounded(rotate(base + low[:, h * 128 : (h + 1) * 128], cos, sin)))
    key = jnp.concatenate([left[:, 512:576], right[:, 512:576]], axis=1) + low[:, 1024:1152]
    value = jnp.concatenate([left[:, 576:640], right[:, 576:640]], axis=1) + low[:, 1152:1280]
    return heads, rounded(rotate(key, cos, sin)), rounded(value)


def split(parity, outs, key, value):
    low = jnp.concatenate(outs[:4] + [key[:, :64], value[:, :64]], axis=1)
    high = jnp.concatenate(outs[4:] + [key[:, 64:], value[:, 64:]], axis=1)
    return sides(parity, low, high)


def attend_kernel(
    plan_ref, parity_ref, used_ref, low_ref, mine_ref, other_ref, cos_ref, sin_ref, key_hbm, value_hbm,
    keep_ref, give_ref, rows_ref, query_ref, near_ref, fresh_ref, out_ref, key_ref, value_ref, sems,
):
    copies = []
    for g in range(4):
        hbm, ref = ((key_hbm, key_ref), (value_hbm, value_ref))[g // 2]
        part = pl.ds((g % 2) * 16, 16)
        copies.append(pltpu.make_async_copy(hbm.at[part], ref.at[part], sems.at[g]))
        copies[-1].start()
    parity = parity_ref[0]
    for i in range(32):
        rows_ref[i : i + 1, :] = low_ref[plan_ref[2 * i + parity]]
    heads, key, value = project(
        parity, mine_ref[...], other_ref[...], rows_ref[...], cos_ref[...], sin_ref[...]
    )
    for h in range(8):
        query_ref[pl.ds(h, 32, 8), :] = heads[h]
        near_ref[pl.ds(h, 32, 8), :] = key
        fresh_ref[pl.ds(h, 32, 8), :] = value
    scale = 1.0 / math.sqrt(HEAD)
    halves = []
    for half in range(2):
        rows = slice(half * 128, (half + 1) * 128)
        query = query_ref[rows, :]
        own = jnp.sum(query * near_ref[rows, :], axis=1, keepdims=True) * scale
        copies[half].wait()
        scores = jnp.concatenate(
            [dot_nt(query[s * 8 : s * 8 + 8].astype(BF16), key_ref[half * 16 + s]) for s in range(16)], axis=0
        ) * scale
        valid = lax.broadcasted_iota(jnp.int32, (128, 512), 1) < used_ref[rows, :]
        top = jnp.max(jnp.where(valid, scores, -jnp.inf), axis=1, keepdims=True)
        top = jnp.maximum(top, own)
        weights = jnp.where(valid, jnp.exp(scores - top), 0.0)
        own_weight = jnp.exp(own - top)
        total = jnp.sum(weights, axis=1, keepdims=True) + own_weight
        halves.append((weights.astype(BF16), own_weight, total))
    for half in range(2):
        copies[2 + half].wait()
        weights, own_weight, total = halves[half]
        rows = slice(half * 128, (half + 1) * 128)
        own = own_weight.astype(BF16).astype(F32) * fresh_ref[rows, :]
        out = jnp.concatenate(
            [dot(weights[s * 8 : s * 8 + 8], value_ref[half * 16 + s]) for s in range(16)], axis=0
        )
        out_ref[rows, :] = (out + own) / total
    outs = [out_ref[pl.ds(h, 32, 8), :] for h in range(8)]
    keep, give = split(parity, outs, key, value)
    keep_ref[...] = keep.astype(BF16)
    give_ref[...] = give.astype(BF16)


def attend_all(plan, parity, used, low, mine, other, cos, sin, keys, values):
    return pl.pallas_call(
        attend_kernel,
        out_shape=[jax.ShapeDtypeStruct((32, 640), BF16)] * 2,
        in_specs=[SMEM] * 2 + [VMEM] * 6 + [ANY] * 2,
        out_specs=[VMEM] * 2,
        scratch_shapes=[
            pltpu.VMEM((32, 1280), F32),
            pltpu.VMEM((256, 128), F32),
            pltpu.VMEM((256, 128), F32),
            pltpu.VMEM((256, 128), F32),
            pltpu.VMEM((256, 128), F32),
            pltpu.VMEM(keys.shape, BF16),
            pltpu.VMEM(values.shape, BF16),
            pltpu.SemaphoreType.DMA((4,)),
        ],
        cost_estimate=pl.CostEstimate(flops=70_000_000, bytes_accessed=1_000_000, transcendentals=131_072),
        compiler_params=pltpu.CompilerParams(vmem_limit_bytes=20 * 2**20),
        name="attend_all",
    )(plan, parity, used, low, mine, other, cos, sin, keys, values)


def amend_kernel(
    plan_ref, parity_ref, used_ref, row_ref, mine_ref, other_ref, cos_ref, sin_ref, key_ref, value_ref,
    keep_in, give_in, keep_ref, give_ref, query_ref,
):
    parity = parity_ref[0]
    first, last = plan_ref[64], plan_ref[65]
    here = ((first & 1) == parity) & ((last & 1) == parity)
    i = last >> 1
    one = pl.ds(i, 1)
    heads, key, value = project(
        parity, mine_ref[one, :], other_ref[one, :], row_ref[0:1, :], cos_ref[one, :], sin_ref[one, :]
    )
    for h in range(8):
        query_ref[h : h + 1, :] = heads[h]
    out = attend(query_ref[...], key, value, key_ref[...], value_ref[...], used_ref[last])
    keep, give = split(parity, [out[h : h + 1] for h in range(8)], key, value)
    hit = (lax.broadcasted_iota(jnp.int32, (32, 640), 0) == i) & here
    keep_ref[...] = jnp.where(hit, keep, keep_in[...].astype(F32)).astype(BF16)
    give_ref[...] = jnp.where(hit, give, give_in[...].astype(F32)).astype(BF16)


def amend(plan, parity, used, row, mine, other, cos, sin, keys, values, keep, give):
    return pl.pallas_call(
        amend_kernel,
        out_shape=[jax.ShapeDtypeStruct((32, 640), BF16)] * 2,
        in_specs=[SMEM] * 3 + [VMEM] * 9,
        out_specs=[VMEM] * 2,
        scratch_shapes=[pltpu.VMEM((8, 128), F32)],
        cost_estimate=pl.CostEstimate(flops=2_000_000, bytes_accessed=500_000, transcendentals=4096),
        compiler_params=pltpu.CompilerParams(vmem_limit_bytes=4 * 2**20),
        name="amend",
    )(plan, parity, used, row, mine, other, cos, sin, keys, values, keep, give)


def pick_kernel(plan_ref, low_ref, row_ref):
    row_ref[...] = low_ref[plan_ref[plan_ref[64]]]


def pick(plan, low):
    return pl.pallas_call(
        pick_kernel,
        out_shape=jax.ShapeDtypeStruct((1, 1280), F32),
        in_specs=[SMEM, VMEM],
        out_specs=VMEM,
        compiler_params=pltpu.CompilerParams(vmem_limit_bytes=2 * 2**20),
        name="pick",
    )(plan, low)


def weave_kernel(parity_ref, keep_ref, back_ref, out_ref, key_ref, value_ref, rows_ref):
    even, odd = sides(parity_ref[0], keep_ref[...].astype(F32), back_ref[...].astype(F32))
    for c in range(5):
        cols = slice(c * 128, (c + 1) * 128)
        rows_ref[pl.ds(0, 32, 2), :] = even[:, cols]
        rows_ref[pl.ds(1, 32, 2), :] = odd[:, cols]
        both = rows_ref[...].astype(BF16)
        if c < 4:
            out_ref[:, cols] = both
        else:
            key_ref[...] = both[:, 0:64]
            value_ref[...] = both[:, 64:128]


def weave(parity, keep, back):
    return pl.pallas_call(
        weave_kernel,
        out_shape=[
            jax.ShapeDtypeStruct((64, 512), BF16),
            jax.ShapeDtypeStruct((64, 64), BF16),
            jax.ShapeDtypeStruct((64, 64), BF16),
        ],
        in_specs=[SMEM, VMEM, VMEM],
        out_specs=[VMEM] * 3,
        scratch_shapes=[pltpu.VMEM((64, 128), F32)],
        compiler_params=pltpu.CompilerParams(vmem_limit_bytes=2 * 2**20),
        name="weave",
    )(parity, keep, back)


def local(
    hidden, wq, wk, wv, down_maps, up_maps, key_cache, value_cache, filled, positions, requests, slots
):
    t = lax.axis_index("tensor")
    parity = t & 1
    z, y = t & 3, t >> 2
    swap = [(i, i ^ 1) for i in range(16)]

    def z_turn(k):
        return [(4 * a + b, 4 * a + (b + k) % 4) for a in range(4) for b in range(4)]

    def y_turn(k):
        return [(4 * a + b, 4 * ((a + k) % 4) + b) for a in range(4) for b in range(4)]

    plan, spread, code, down_near, up_near, hidden_near = make_plan(
        z.reshape(1), requests, slots, hidden, down_maps.reshape(96, 8192), up_maps.reshape(32, 10240)
    )
    around_z = [hidden_near] + [lax.ppermute(hidden, "tensor", z_turn(k)) for k in (1, 2, 3)]
    sent = send_rows(spread, code, around_z)
    rings = [[g * 16 + a * 4 + b for a in range(4) for g in range(8)] for b in range(4)]
    recv = lax.all_to_all(sent, ("dp", "tensor"), 0, 0, tiled=True, axis_index_groups=rings)
    band = stack_band(plan, around_z)
    up, down = (lax.ppermute(band, "tensor", y_turn(k)) for k in (1, 3))

    halves = take_halves(up, down)
    halves = [lax.ppermute(half, "tensor", y_turn(k)) for half, k in zip(halves, (1, 3))]
    recv, up, down = lax.optimization_barrier((recv, up, down))
    low_sent = owner_low(z.reshape(1), recv, down_near, up_near)
    low_sent, *halves = lax.optimization_barrier((low_sent, *halves))
    low = lax.all_to_all(low_sent, ROUTE, 0, 0, tiled=True)

    place = jnp.stack([y, z]).astype(jnp.int32)
    mine, give, key2, value2 = base_project(
        place, plan, (band, up, *halves, down), wq, wk.T, wv.T, key_cache[0], value_cache[0], low_sent
    )
    other = lax.ppermute(give, "tensor", swap)

    positions, filled, mine = lax.optimization_barrier((positions, filled, mine))
    pos = lax.dynamic_index_in_dim(positions.reshape(32, 2), parity, 1, keepdims=False)
    freq = THETA ** (-2.0 * jnp.arange(64, dtype=F32) / HEAD)
    angle = pos.astype(F32)[:, None] * freq[None, :]
    cos, sin = jnp.cos(angle), jnp.sin(angle)
    cos, sin = jnp.concatenate([cos, cos], 1), jnp.concatenate([-sin, sin], 1)

    which = parity.reshape(1)
    row = lax.ppermute(pick(plan, low), "tensor", swap)
    keys, values = in_hbm(key_cache[0], value_cache[0])
    used = lax.dynamic_index_in_dim(filled.reshape(32, 2), parity, 1, keepdims=False)
    used = jnp.repeat(used, 8).reshape(256, 1)
    keep, give = attend_all(plan, which, used, low, mine, other, cos, sin, keys, values)
    keep, give = amend(
        plan, which, filled, row, mine, other, cos, sin, key2, value2, keep, give
    )
    back = lax.ppermute(give, "tensor", swap)
    return tuple(weave(which, keep, back))


def solution(mesh):
    return jax.shard_map(
        local,
        mesh=mesh,
        in_specs=(
            P("dp", "tensor"),
            P(None, "tensor"),
            P(None, "tensor"),
            P(None, "tensor"),
            P(("dp", "tensor"), None, None),
            P(("dp", "tensor"), None, None),
            P("tensor", "dp", None, None),
            P("tensor", "dp", None, None),
            P("dp"),
            P("dp"),
            P("dp", None),
            P("dp"),
        ),
        out_specs=(P("dp", "tensor"), P("dp", "tensor"), P("dp", "tensor")),
        check_vma=False,
    )
```

```python
import functools
import math

import jax
import jax.numpy as jnp
from jax import lax
from jax.experimental import pallas as pl
from jax.experimental.pallas import tpu as pltpu
from jax.sharding import PartitionSpec as P

HEAD = 128
RANK = 8
THETA = 500000.0
ROUTE = ("tensor", "dp")
BF16 = jnp.bfloat16
F32 = jnp.float32
SMEM = pl.BlockSpec(memory_space=pltpu.SMEM)
VMEM = pl.BlockSpec(memory_space=pltpu.VMEM)
ANY = pl.BlockSpec(memory_space=pl.ANY)
NT = (((1,), (1,)), ((), ()))
dot = functools.partial(jnp.dot, preferred_element_type=F32)
dot_nt = functools.partial(lax.dot_general, dimension_numbers=NT, preferred_element_type=F32)


def plan_kernel(
    z_ref, requests_hbm, slots_hbm, hidden_hbm, down_hbm, up_hbm, key_hbm, value_hbm,
    plan_ref, spread_ref, code_ref, down_ref, up_ref, hidden_ref, pair_ref,
    eye_ref, wide_ref, requests_ref, slots_ref, sems,
):
    copies = [
        pltpu.make_async_copy(requests_hbm, requests_ref, sems.at[0]),
        pltpu.make_async_copy(slots_hbm, slots_ref, sems.at[1]),
    ]
    near = [
        pltpu.make_async_copy(hidden_hbm, hidden_ref, sems.at[2]),
        pltpu.make_async_copy(down_hbm, down_ref, sems.at[3]),
        pltpu.make_async_copy(up_hbm, up_ref, sems.at[4]),
    ]
    for copy in copies + near:
        copy.start()
    spread_ref[...] = jnp.zeros_like(spread_ref)
    code_ref[...] = jnp.zeros_like(code_ref)
    shape = eye_ref.shape
    rows, cols = (lax.broadcasted_iota(jnp.int32, shape, d) for d in range(2))
    eye_ref[...] = jnp.where(rows == cols, 1.0, 0.0)
    for copy in copies:
        copy.wait()
    z = z_ref[0]
    first = jnp.int32(-1)
    last = jnp.int32(-1)
    for s in range(64):
        slot = slots_ref[s]
        adapter = requests_ref[0, slot]
        owner = adapter >> 2
        place = (owner & 15) * 8 + (owner >> 4)
        plan_ref[s] = place
        zero = slot == 0
        rank = jnp.where(zero & (first >= 0), 1, 0)
        last = jnp.where(zero, s, last)
        first = jnp.where(zero & (first < 0), s, first)
        code = ((adapter & 3) + 4 * (s % 2)).astype(F32)
        wide_ref[s : s + 1, :] = jnp.full((1, 128), code, F32)
        row = pl.ds(((place >> 5) * 8 + (place & 7)) * 2 + rank, 1)

        @pl.when(((place >> 3) & 3) == z)
        def _():
            spread_ref[row, :] = eye_ref[s : s + 1, :]
            code_ref[row, :] = wide_ref[s : s + 1, :]

    plan_ref[64] = first
    plan_ref[65] = last
    column = jnp.maximum(last, 0) >> 1
    cache = [
        pltpu.make_async_copy(key_hbm.at[column], pair_ref.at[0], sems.at[5]),
        pltpu.make_async_copy(value_hbm.at[column], pair_ref.at[1], sems.at[6]),
    ]
    for copy in cache:
        copy.start()
    for copy in near + cache:
        copy.wait()


def in_hbm(*arrays):
    return [pltpu.with_memory_space_constraint(x, pltpu.HBM) for x in arrays]


def make_plan(z, requests, slots, hidden, down, up, keys, values):
    return pl.pallas_call(
        plan_kernel,
        out_shape=[
            jax.ShapeDtypeStruct((66,), jnp.int32),
            jax.ShapeDtypeStruct((64, 128), F32),
            jax.ShapeDtypeStruct((64, 128), F32),
            pltpu.VMEM(down.shape, BF16),
            pltpu.VMEM(up.shape, BF16),
            pltpu.VMEM(hidden.shape, BF16),
            jax.ShapeDtypeStruct((2,) + keys.shape[1:], BF16),
        ],
        in_specs=[SMEM] + [ANY] * 7,
        out_specs=[SMEM, VMEM, VMEM, ANY, ANY, VMEM, VMEM],
        scratch_shapes=[
            pltpu.VMEM((64, 128), F32),
            pltpu.VMEM((64, 128), F32),
            pltpu.SMEM((1, 63), jnp.int32),
            pltpu.SMEM((64,), jnp.int32),
            pltpu.SemaphoreType.DMA((7,)),
        ],
        cost_estimate=pl.CostEstimate(flops=1_000_000, bytes_accessed=500_000, transcendentals=0),
        compiler_params=pltpu.CompilerParams(vmem_limit_bytes=4 * 2**20),
        name="make_plan",
    )(z, *in_hbm(requests, slots, hidden, down, up, keys, values))


def send_kernel(spread_ref, code_ref, h0_ref, h1_ref, h2_ref, h3_ref, sent_ref):
    spread = spread_ref[:, 0:64].astype(BF16)
    for k, ref in enumerate((h0_ref, h1_ref, h2_ref, h3_ref)):
        rows = dot(spread, ref[...])
        sent_ref[:, :, k * 512 : (k + 1) * 512] = rows.reshape(32, 2, 512).astype(BF16)
    sent_ref[:, :, 2048:2176] = code_ref[...].reshape(32, 2, 128).astype(BF16)


def send_rows(spread, code, blocks):
    return pl.pallas_call(
        send_kernel,
        out_shape=pltpu.HBM((32, 2, 2176), BF16),
        in_specs=[VMEM] * 6,
        out_specs=VMEM,
        cost_estimate=pl.CostEstimate(flops=1_000_000, bytes_accessed=500_000, transcendentals=0),
        compiler_params=pltpu.CompilerParams(vmem_limit_bytes=4 * 2**20),
        name="send_rows",
    )(spread, code, *blocks)


def band_kernel(_, h0_ref, h1_ref, h2_ref, h3_ref, out_ref):
    for k, ref in enumerate((h0_ref, h1_ref, h2_ref, h3_ref)):
        out_ref[k] = ref[...]


def stack_band(plan, blocks):
    return pl.pallas_call(
        band_kernel,
        out_shape=jax.ShapeDtypeStruct((4, 64, 512), BF16),
        in_specs=[SMEM] + [VMEM] * 4,
        out_specs=VMEM,
        cost_estimate=pl.CostEstimate(flops=1000, bytes_accessed=500_000, transcendentals=0),
        compiler_params=pltpu.CompilerParams(vmem_limit_bytes=4 * 2**20),
        name="stack_band",
    )(plan, *blocks)


def halves_kernel(up_ref, down_ref, a_ref, b_ref):
    a_ref[...] = up_ref[0:2]
    b_ref[...] = down_ref[2:4]


def take_halves(up, down):
    return pl.pallas_call(
        halves_kernel,
        out_shape=[jax.ShapeDtypeStruct((2, 64, 512), BF16)] * 2,
        in_specs=[VMEM] * 2,
        out_specs=[VMEM] * 2,
        cost_estimate=pl.CostEstimate(flops=1000, bytes_accessed=500_000, transcendentals=0),
        compiler_params=pltpu.CompilerParams(vmem_limit_bytes=4 * 2**20),
        name="take_halves",
    )(up, down)


def owner_kernel(z_ref, recv_ref, down_ref, up_ref, out_ref, coords_ref, code_ref):
    z = z_ref[0]
    acc = jnp.zeros((16, 96), F32)
    for y in range(4):
        for k in range(4):
            rows = recv_ref[y * 8 : (y + 1) * 8, :, k * 512 : (k + 1) * 512].reshape(16, 512)
            cols = pl.ds(pl.multiple_of((4 * y + ((z - k) & 3)) * 512, 512), 512)
            acc = acc + dot_nt(rows, down_ref[:, cols])
    coords_ref[:, 0:96] = acc.astype(BF16).astype(F32)
    code_ref[...] = recv_ref[0:8, :, 2048:2176].reshape(16, 128).astype(F32)
    one, two = coords_ref[pl.ds(0, 8, 2), :], coords_ref[pl.ds(1, 8, 2), :]
    code = code_ref[pl.ds(0, 8, 2), :][:, 0:1].astype(jnp.int32)
    odd = code >= 4
    coords = jnp.concatenate([jnp.where(odd, two, one), jnp.where(odd, one, two)], axis=0)
    ids = jnp.concatenate([code, code], axis=0) & 3
    mine = (lax.broadcasted_iota(jnp.int32, (16, 32), 1) >> 3) == ids
    blocks = []
    for b in range(3):
        block = jnp.concatenate(
            [coords[:, a * 24 + b * 8 : a * 24 + b * 8 + 8] for a in range(4)], axis=1
        )
        blocks.append(jnp.where(mine, block, 0.0).astype(BF16))
    low_key = dot(blocks[1], up_ref[:, 8192:9216])
    low_value = dot(blocks[2], up_ref[:, 9216:10240])
    for j in range(8):
        low_query = dot(blocks[0], up_ref[:, j * 1024 : (j + 1) * 1024])
        head = slice(j * 128, (j + 1) * 128)
        for p in range(2):
            rows, half = slice((2 * j + p) * 8, (2 * j + p + 1) * 8), slice(p * 8, p * 8 + 8)
            out_ref[rows, 0, 0:1024] = low_query[half]
            out_ref[rows, 0, 1024:1152] = low_key[half, head]
            out_ref[rows, 0, 1152:1280] = low_value[half, head]


def owner_low(z, recv, down, up):
    return pl.pallas_call(
        owner_kernel,
        out_shape=jax.ShapeDtypeStruct((128, 1, 1280), F32),
        in_specs=[SMEM] + [VMEM] * 3,
        out_specs=VMEM,
        scratch_shapes=[
            pltpu.VMEM((16, 128), F32),
            pltpu.VMEM((16, 128), F32),
        ],
        cost_estimate=pl.CostEstimate(flops=40_000_000, bytes_accessed=3_400_000, transcendentals=0),
        compiler_params=pltpu.CompilerParams(vmem_limit_bytes=8 * 2**20),
        name="owner_low",
    )(z, recv, down, up)


def weight_copies(rows, wq_hbm, wk_hbm, wv_hbm, wq_ref, wkv_ref, sems):
    copies = []
    for i, row in enumerate(rows):
        part = pl.ds(pl.multiple_of(row, 512), 512)
        copies.append(
            [
                pltpu.make_async_copy(wk_hbm.at[:, part], wkv_ref.at[i, 0:64], sems.at[0, i]),
                pltpu.make_async_copy(wv_hbm.at[:, part], wkv_ref.at[i, 64:128], sems.at[1, i]),
                pltpu.make_async_copy(wq_hbm.at[part], wq_ref.at[i], sems.at[2, i]),
            ]
        )
    for block in copies:
        for copy in block:
            copy.start()
    return copies


def add_blocks(hiddens, copies, wq_ref, wkv_ref, q, kv):
    for i, hidden in enumerate(hiddens):
        for copy in copies[i]:
            copy.wait()
        q = q + dot(hidden, wq_ref[i])
        kv = kv + dot_nt(hidden, wkv_ref[i])
    return q, kv


def base_kernel(
    place_ref, plan_ref, h0_ref, h1_ref, ha_ref, hb_ref, h3_ref, wq_hbm, wk_hbm, wv_hbm, _,
    mine_ref, give_ref, wq_ref, wkv_ref, acc_ref, sems,
):
    y, z = place_ref[0], place_ref[1]
    rows = [(((y - a) & 3) * 4 + ((z - b) & 3)) * 512 for a in range(4) for b in range(4)]
    copies = weight_copies(rows, wq_hbm, wk_hbm, wv_hbm, wq_ref, wkv_ref, sems)
    hiddens = [ref[b] for ref in (h0_ref, h1_ref) for b in range(4)]
    hiddens += [ha_ref[0], ha_ref[1], hb_ref[0], hb_ref[1]] + [h3_ref[b] for b in range(4)]
    q, kv = jnp.zeros((64, 512), F32), jnp.zeros((64, 128), F32)
    for i, hidden in enumerate(hiddens):
        for copy in copies[i]:
            copy.wait()
        q = q + dot(hidden, wq_ref[i])
        kv = kv + dot_nt(hidden, wkv_ref[i])
    parity = z & 1
    for c in range(5):
        cols = slice(c * 128, (c + 1) * 128)
        acc_ref[...] = q[:, cols] if c < 4 else kv
        even, odd = acc_ref[pl.ds(0, 32, 2), :], acc_ref[pl.ds(1, 32, 2), :]
        mine_ref[0:32, cols], give_ref[0:32, cols] = sides(parity, even, odd)
    row = pl.ds(plan_ref[65] >> 1, 1)
    mine_ref[32:40, :] = jnp.broadcast_to(give_ref[row, :], (8, 640))
    give_ref[32:40, :] = jnp.broadcast_to(mine_ref[row, :], (8, 640))


def base_project(place, plan, bands, wq, wkt, wvt, after):
    return pl.pallas_call(
        base_kernel,
        out_shape=[
            jax.ShapeDtypeStruct((40, 640), F32),
            jax.ShapeDtypeStruct((40, 640), F32),
        ],
        in_specs=[SMEM] * 2 + [VMEM] * 5 + [ANY] * 4,
        out_specs=[VMEM] * 2,
        scratch_shapes=[
            pltpu.VMEM((16, 512, 512), BF16),
            pltpu.VMEM((16, 128, 512), BF16),
            pltpu.VMEM((64, 128), F32),
            pltpu.SemaphoreType.DMA((3, 16)),
        ],
        cost_estimate=pl.CostEstimate(flops=671_000_000, bytes_accessed=11_700_000, transcendentals=0),
        compiler_params=pltpu.CompilerParams(vmem_limit_bytes=16 * 2**20),
        name="base_project",
    )(place, plan, *bands, *in_hbm(wq, wkt, wvt), after)


def rotate(part, cos, sin):
    return part * cos + pltpu.roll(part, 64, 1) * sin


def sides(parity, mine, other):
    even = parity == 0
    return jnp.where(even, mine, other), jnp.where(even, other, mine)


def project(parity, mine, other, low, cos, sin):
    def rounded(x):
        return x.astype(BF16).astype(F32)

    left, right = sides(parity, mine, other)
    heads = []
    for h in range(8):
        base = (left if h < 4 else right)[:, (h % 4) * 128 : (h % 4 + 1) * 128]
        heads.append(rounded(rotate(base + low[:, h * 128 : (h + 1) * 128], cos, sin)))
    key = jnp.concatenate([left[:, 512:576], right[:, 512:576]], axis=1) + low[:, 1024:1152]
    value = jnp.concatenate([left[:, 576:640], right[:, 576:640]], axis=1) + low[:, 1152:1280]
    return heads, rounded(rotate(key, cos, sin)), rounded(value)


def split(parity, outs, key, value):
    low = jnp.concatenate(outs[:4] + [key[:, :64], value[:, :64]], axis=1)
    high = jnp.concatenate(outs[4:] + [key[:, 64:], value[:, 64:]], axis=1)
    return sides(parity, low, high)


def attend_kernel(
    plan_ref, parity_ref, filled_ref, low_ref, mine_ref, other_ref, cos_ref, sin_ref, pair_ref, key_hbm, value_hbm,
    keep_ref, give_ref, rows_ref, query_ref, near_ref, fresh_ref, out_ref, key_ref, value_ref, sems,
):
    copies = []
    for g in range(4):
        hbm, ref = ((key_hbm, key_ref), (value_hbm, value_ref))[g // 2]
        part = pl.ds((g % 2) * 16, 16)
        copies.append(pltpu.make_async_copy(hbm.at[part], ref.at[part], sems.at[g]))
        copies[-1].start()
    parity = parity_ref[0]
    for i in range(32):
        rows_ref[i : i + 1, :] = low_ref[plan_ref[2 * i + parity]]
    rows_ref[32:40, :] = jnp.broadcast_to(low_ref[plan_ref[plan_ref[64]]], (8, 1280))
    last = plan_ref[65]

    def table(ref):
        mine = jnp.where(parity == 0, ref[pl.ds(0, 32, 2), :], ref[pl.ds(1, 32, 2), :])
        more = jnp.broadcast_to(ref[pl.ds(last, 1), :], (8, 128))
        return jnp.concatenate([mine, more], axis=0)

    heads, key, value = project(
        parity, mine_ref[...], other_ref[...], rows_ref[...], table(cos_ref), table(sin_ref)
    )
    for h in range(8):
        query_ref[pl.ds(h, 40, 8), :] = heads[h]
        near_ref[pl.ds(h, 40, 8), :] = key
        fresh_ref[pl.ds(h, 40, 8), :] = value
    scale = 1.0 / math.sqrt(HEAD)
    def caches(half, ref, which):
        return [ref[half * 16 + s] for s in range(16)] + ([pair_ref[which]] if half else [])

    halves = []
    for half in range(2):
        rows = slice(half * 128, half * 136 + 128)
        query = query_ref[rows, :]
        own = jnp.sum(query * near_ref[rows, :], axis=1, keepdims=True) * scale
        copies[half].wait()
        scores = jnp.concatenate(
            [
                dot_nt(query[s * 8 : s * 8 + 8].astype(BF16), block)
                for s, block in enumerate(caches(half, key_ref, 0))
            ],
            axis=0,
        ) * scale
        used = [filled_ref[2 * (half * 16 + s) + parity] for s in range(16)] + [filled_ref[last]] * half
        slot = lax.broadcasted_iota(jnp.int32, (8, 512), 1)
        left = jnp.concatenate([n - slot for n in used], axis=0)
        valid = left > 0
        top = jnp.max(jnp.where(valid, scores, -jnp.inf), axis=1, keepdims=True)
        top = jnp.maximum(top, own)
        weights = jnp.where(valid, jnp.exp(scores - top), 0.0)
        own_weight = jnp.exp(own - top)
        total = jnp.sum(weights, axis=1, keepdims=True) + own_weight
        halves.append((weights.astype(BF16), own_weight, total))
    for half in range(2):
        copies[2 + half].wait()
        weights, own_weight, total = halves[half]
        rows = slice(half * 128, half * 136 + 128)
        own = own_weight.astype(BF16).astype(F32) * fresh_ref[rows, :]
        out = jnp.concatenate(
            [
                dot(weights[s * 8 : s * 8 + 8], block)
                for s, block in enumerate(caches(half, value_ref, 1))
            ],
            axis=0,
        )
        out_ref[rows, :] = (out + own) / total
    outs = [out_ref[pl.ds(h, 40, 8), :] for h in range(8)]
    keep, give = split(parity, outs, key, value)
    keep_ref[...] = keep.astype(BF16)
    give_ref[...] = give.astype(BF16)


def attend_all(plan, parity, filled, low, mine, other, cos, sin, pair, keys, values):
    return pl.pallas_call(
        attend_kernel,
        out_shape=[jax.ShapeDtypeStruct((40, 640), BF16)] * 2,
        in_specs=[SMEM] * 3 + [VMEM] * 6 + [ANY] * 2,
        out_specs=[VMEM] * 2,
        scratch_shapes=[
            pltpu.VMEM((40, 1280), F32),
            pltpu.VMEM((320, 128), F32),
            pltpu.VMEM((320, 128), F32),
            pltpu.VMEM((320, 128), F32),
            pltpu.VMEM((320, 128), F32),
            pltpu.VMEM(keys.shape, BF16),
            pltpu.VMEM(values.shape, BF16),
            pltpu.SemaphoreType.DMA((4,)),
        ],
        cost_estimate=pl.CostEstimate(flops=70_000_000, bytes_accessed=1_000_000, transcendentals=131_072),
        compiler_params=pltpu.CompilerParams(vmem_limit_bytes=20 * 2**20),
        name="attend_all",
    )(plan, parity, filled, low, mine, other, cos, sin, pair, keys, values)


def weave_kernel(plan_ref, parity_ref, keep_ref, back_ref, out_ref, key_ref, value_ref, rows_ref, extra_ref):
    parity, first, last = parity_ref[0], plan_ref[64], plan_ref[65]
    keep, back = keep_ref[...].astype(F32), back_ref[...].astype(F32)
    even, odd = sides(parity, keep[0:32], back[0:32])
    extra_ref[...] = jnp.where(parity == (last & 1), back[32:40], keep[32:40])
    same = (first & 1) == (last & 1)
    for c in range(5):
        cols = slice(c * 128, (c + 1) * 128)
        rows_ref[pl.ds(0, 32, 2), :] = even[:, cols]
        rows_ref[pl.ds(1, 32, 2), :] = odd[:, cols]

        @pl.when(same)
        def _():
            rows_ref[pl.ds(last, 1), :] = extra_ref[0:1, cols]

        both = rows_ref[...].astype(BF16)
        if c < 4:
            out_ref[:, cols] = both
        else:
            key_ref[...] = both[:, 0:64]
            value_ref[...] = both[:, 64:128]


def weave(plan, parity, keep, back):
    return pl.pallas_call(
        weave_kernel,
        out_shape=[
            jax.ShapeDtypeStruct((64, 512), BF16),
            jax.ShapeDtypeStruct((64, 64), BF16),
            jax.ShapeDtypeStruct((64, 64), BF16),
        ],
        in_specs=[SMEM, SMEM, VMEM, VMEM],
        out_specs=[VMEM] * 3,
        scratch_shapes=[pltpu.VMEM((64, 128), F32), pltpu.VMEM((8, 640), F32)],
        compiler_params=pltpu.CompilerParams(vmem_limit_bytes=2 * 2**20),
        name="weave",
    )(plan, parity, keep, back)


def local(
    hidden, wq, wk, wv, down_maps, up_maps, key_cache, value_cache, filled, positions, requests, slots
):
    t = lax.axis_index("tensor")
    parity = t & 1
    z, y = t & 3, t >> 2
    swap = [(i, i ^ 1) for i in range(16)]

    def z_turn(k):
        return [(4 * a + b, 4 * a + (b + k) % 4) for a in range(4) for b in range(4)]

    def y_turn(k):
        return [(4 * a + b, 4 * ((a + k) % 4) + b) for a in range(4) for b in range(4)]

    plan, spread, code, down_near, up_near, hidden_near, pair = make_plan(
        z.reshape(1), requests, slots, hidden, down_maps.reshape(96, 8192), up_maps.reshape(32, 10240),
        key_cache[0], value_cache[0],
    )
    around_z = [hidden_near] + [lax.ppermute(hidden, "tensor", z_turn(k)) for k in (1, 2, 3)]
    sent = send_rows(spread, code, around_z)
    rings = [[g * 16 + a * 4 + b for a in range(4) for g in range(8)] for b in range(4)]
    recv = lax.all_to_all(sent, ("dp", "tensor"), 0, 0, tiled=True, axis_index_groups=rings)
    band = stack_band(plan, around_z)
    up, down = (lax.ppermute(band, "tensor", y_turn(k)) for k in (1, 3))

    halves = take_halves(up, down)
    halves = [lax.ppermute(half, "tensor", y_turn(k)) for half, k in zip(halves, (1, 3))]
    pair = lax.ppermute(pair, "tensor", swap)
    recv, up, down = lax.optimization_barrier((recv, up, down))
    low_sent = owner_low(z.reshape(1), recv, down_near, up_near)
    low_sent, pair, *halves = lax.optimization_barrier((low_sent, pair, *halves))
    low = lax.all_to_all(low_sent, ROUTE, 0, 0, tiled=True)

    place = jnp.stack([y, z]).astype(jnp.int32)
    mine, give = base_project(place, plan, (band, up, *halves, down), wq, wk.T, wv.T, low_sent)
    other = lax.ppermute(give, "tensor", swap)

    pos, mine = lax.optimization_barrier((positions, mine))
    freq = THETA ** (-2.0 * jnp.arange(64, dtype=F32) / HEAD)
    angle = pos.astype(F32)[:, None] * freq[None, :]
    cos, sin = jnp.cos(angle), jnp.sin(angle)
    cos, sin = jnp.concatenate([cos, cos], 1), jnp.concatenate([-sin, sin], 1)

    which = parity.reshape(1)
    keys, values = in_hbm(key_cache[0], value_cache[0])
    keep, give = attend_all(plan, which, filled, low, mine, other, cos, sin, pair, keys, values)
    back = lax.ppermute(give, "tensor", swap)
    return tuple(weave(plan, which, keep, back))


def solution(mesh):
    return jax.shard_map(
        local,
        mesh=mesh,
        in_specs=(
            P("dp", "tensor"),
            P(None, "tensor"),
            P(None, "tensor"),
            P(None, "tensor"),
            P(("dp", "tensor"), None, None),
            P(("dp", "tensor"), None, None),
            P("tensor", "dp", None, None),
            P("tensor", "dp", None, None),
            P("dp"),
            P("dp"),
            P("dp", None),
            P("dp"),
        ),
        out_specs=(P("dp", "tensor"), P("dp", "tensor"), P("dp", "tensor")),
        check_vma=False,
    )
```

```python
import functools
import math

import jax
import jax.numpy as jnp
from jax import lax
from jax.experimental import pallas as pl
from jax.experimental.pallas import tpu as pltpu
from jax.sharding import PartitionSpec as P

HEAD = 128
RANK = 8
THETA = 500000.0
ROUTE = ("tensor", "dp")
BF16 = jnp.bfloat16
F32 = jnp.float32
SMEM = pl.BlockSpec(memory_space=pltpu.SMEM)
VMEM = pl.BlockSpec(memory_space=pltpu.VMEM)
ANY = pl.BlockSpec(memory_space=pl.ANY)
NT = (((1,), (1,)), ((), ()))
dot = functools.partial(jnp.dot, preferred_element_type=F32)
dot_nt = functools.partial(lax.dot_general, dimension_numbers=NT, preferred_element_type=F32)


def plan_kernel(
    z_ref, requests_hbm, slots_hbm, hidden_hbm, down_hbm, up_hbm, key_hbm, value_hbm,
    plan_ref, spread_ref, code_ref, down_ref, up_ref, hidden_ref, pair_ref,
    eye_ref, wide_ref, requests_ref, slots_ref, sems,
):
    copies = [
        pltpu.make_async_copy(requests_hbm, requests_ref, sems.at[0]),
        pltpu.make_async_copy(slots_hbm, slots_ref, sems.at[1]),
    ]
    near = [
        pltpu.make_async_copy(hidden_hbm, hidden_ref, sems.at[2]),
        pltpu.make_async_copy(down_hbm, down_ref, sems.at[3]),
        pltpu.make_async_copy(up_hbm, up_ref, sems.at[4]),
    ]
    for copy in copies + near:
        copy.start()
    spread_ref[...] = jnp.zeros_like(spread_ref)
    code_ref[...] = jnp.zeros_like(code_ref)
    shape = eye_ref.shape
    rows, cols = (lax.broadcasted_iota(jnp.int32, shape, d) for d in range(2))
    eye_ref[...] = jnp.where(rows == cols, 1.0, 0.0)
    for copy in copies:
        copy.wait()
    z = z_ref[0]
    first = jnp.int32(-1)
    last = jnp.int32(-1)
    for s in range(64):
        slot = slots_ref[s]
        adapter = requests_ref[0, slot]
        owner = adapter >> 2
        place = (owner & 15) * 8 + (owner >> 4)
        plan_ref[s] = place
        zero = slot == 0
        rank = jnp.where(zero & (first >= 0), 1, 0)
        last = jnp.where(zero, s, last)
        first = jnp.where(zero & (first < 0), s, first)
        code = ((adapter & 3) + 4 * (s % 2)).astype(F32)
        wide_ref[s : s + 1, :] = jnp.full((1, 128), code, F32)
        row = pl.ds(((place >> 5) * 8 + (place & 7)) * 2 + rank, 1)

        @pl.when(((place >> 3) & 3) == z)
        def _():
            spread_ref[row, :] = eye_ref[s : s + 1, :]
            code_ref[row, :] = wide_ref[s : s + 1, :]

    plan_ref[64] = first
    plan_ref[65] = last
    column = jnp.maximum(last, 0) >> 1
    cache = [
        pltpu.make_async_copy(key_hbm.at[column], pair_ref.at[0], sems.at[5]),
        pltpu.make_async_copy(value_hbm.at[column], pair_ref.at[1], sems.at[6]),
    ]
    for copy in cache:
        copy.start()
    for copy in near + cache:
        copy.wait()


def in_hbm(*arrays):
    return [pltpu.with_memory_space_constraint(x, pltpu.HBM) for x in arrays]


def make_plan(z, requests, slots, hidden, down, up, keys, values):
    return pl.pallas_call(
        plan_kernel,
        out_shape=[
            jax.ShapeDtypeStruct((66,), jnp.int32),
            jax.ShapeDtypeStruct((64, 128), F32),
            jax.ShapeDtypeStruct((64, 128), F32),
            pltpu.VMEM(down.shape, BF16),
            pltpu.VMEM(up.shape, BF16),
            pltpu.VMEM(hidden.shape, BF16),
            jax.ShapeDtypeStruct((2,) + keys.shape[1:], BF16),
        ],
        in_specs=[SMEM] + [ANY] * 7,
        out_specs=[SMEM, VMEM, VMEM, ANY, ANY, VMEM, VMEM],
        scratch_shapes=[
            pltpu.VMEM((64, 128), F32),
            pltpu.VMEM((64, 128), F32),
            pltpu.SMEM((1, 63), jnp.int32),
            pltpu.SMEM((64,), jnp.int32),
            pltpu.SemaphoreType.DMA((7,)),
        ],
        cost_estimate=pl.CostEstimate(flops=1_000_000, bytes_accessed=500_000, transcendentals=0),
        compiler_params=pltpu.CompilerParams(vmem_limit_bytes=4 * 2**20),
        name="make_plan",
    )(z, *in_hbm(requests, slots, hidden, down, up, keys, values))


def send_kernel(spread_ref, code_ref, h0_ref, h1_ref, h2_ref, h3_ref, sent_ref):
    spread = spread_ref[:, 0:64].astype(BF16)
    for k, ref in enumerate((h0_ref, h1_ref, h2_ref, h3_ref)):
        rows = dot(spread, ref[...])
        sent_ref[:, :, k * 512 : (k + 1) * 512] = rows.reshape(32, 2, 512).astype(BF16)
    sent_ref[:, :, 2048:2176] = code_ref[...].reshape(32, 2, 128).astype(BF16)


def send_rows(spread, code, blocks):
    return pl.pallas_call(
        send_kernel,
        out_shape=pltpu.HBM((32, 2, 2176), BF16),
        in_specs=[VMEM] * 6,
        out_specs=VMEM,
        cost_estimate=pl.CostEstimate(flops=1_000_000, bytes_accessed=500_000, transcendentals=0),
        compiler_params=pltpu.CompilerParams(vmem_limit_bytes=4 * 2**20),
        name="send_rows",
    )(spread, code, *blocks)


def band_kernel(_, h0_ref, h1_ref, h2_ref, h3_ref, out_ref):
    for k, ref in enumerate((h0_ref, h1_ref, h2_ref, h3_ref)):
        out_ref[k] = ref[...]


def stack_band(plan, blocks):
    return pl.pallas_call(
        band_kernel,
        out_shape=jax.ShapeDtypeStruct((4, 64, 512), BF16),
        in_specs=[SMEM] + [VMEM] * 4,
        out_specs=VMEM,
        cost_estimate=pl.CostEstimate(flops=1000, bytes_accessed=500_000, transcendentals=0),
        compiler_params=pltpu.CompilerParams(vmem_limit_bytes=4 * 2**20),
        name="stack_band",
    )(plan, *blocks)


def halves_kernel(up_ref, down_ref, a_ref, b_ref):
    a_ref[...] = up_ref[0:2]
    b_ref[...] = down_ref[2:4]


def take_halves(up, down):
    return pl.pallas_call(
        halves_kernel,
        out_shape=[jax.ShapeDtypeStruct((2, 64, 512), BF16)] * 2,
        in_specs=[VMEM] * 2,
        out_specs=[VMEM] * 2,
        cost_estimate=pl.CostEstimate(flops=1000, bytes_accessed=500_000, transcendentals=0),
        compiler_params=pltpu.CompilerParams(vmem_limit_bytes=4 * 2**20),
        name="take_halves",
    )(up, down)


def owner_kernel(z_ref, recv_ref, down_ref, up_ref, out_ref, coords_ref, code_ref):
    z = z_ref[0]
    acc = jnp.zeros((16, 96), F32)
    for y in range(4):
        for k in range(4):
            rows = recv_ref[y * 8 : (y + 1) * 8, :, k * 512 : (k + 1) * 512].reshape(16, 512)
            cols = pl.ds(pl.multiple_of((4 * y + ((z - k) & 3)) * 512, 512), 512)
            acc = acc + dot_nt(rows, down_ref[:, cols])
    coords_ref[:, 0:96] = acc.astype(BF16).astype(F32)
    code_ref[...] = recv_ref[0:8, :, 2048:2176].reshape(16, 128).astype(F32)
    one, two = coords_ref[pl.ds(0, 8, 2), :], coords_ref[pl.ds(1, 8, 2), :]
    code = code_ref[pl.ds(0, 8, 2), :][:, 0:1].astype(jnp.int32)
    odd = code >= 4
    coords = jnp.concatenate([jnp.where(odd, two, one), jnp.where(odd, one, two)], axis=0)
    ids = jnp.concatenate([code, code], axis=0) & 3
    mine = (lax.broadcasted_iota(jnp.int32, (16, 32), 1) >> 3) == ids
    blocks = []
    for b in range(3):
        block = jnp.concatenate(
            [coords[:, a * 24 + b * 8 : a * 24 + b * 8 + 8] for a in range(4)], axis=1
        )
        blocks.append(jnp.where(mine, block, 0.0).astype(BF16))
    low_key = dot(blocks[1], up_ref[:, 8192:9216])
    low_value = dot(blocks[2], up_ref[:, 9216:10240])
    for j in range(8):
        low_query = dot(blocks[0], up_ref[:, j * 1024 : (j + 1) * 1024])
        head = slice(j * 128, (j + 1) * 128)
        for p in range(2):
            rows, half = slice((2 * j + p) * 8, (2 * j + p + 1) * 8), slice(p * 8, p * 8 + 8)
            out_ref[rows, 0, 0:1024] = low_query[half]
            out_ref[rows, 0, 1024:1152] = low_key[half, head]
            out_ref[rows, 0, 1152:1280] = low_value[half, head]


def owner_low(z, recv, down, up):
    return pl.pallas_call(
        owner_kernel,
        out_shape=jax.ShapeDtypeStruct((128, 1, 1280), F32),
        in_specs=[SMEM] + [VMEM] * 3,
        out_specs=VMEM,
        scratch_shapes=[
            pltpu.VMEM((16, 128), F32),
            pltpu.VMEM((16, 128), F32),
        ],
        cost_estimate=pl.CostEstimate(flops=40_000_000, bytes_accessed=3_400_000, transcendentals=0),
        compiler_params=pltpu.CompilerParams(vmem_limit_bytes=8 * 2**20),
        name="owner_low",
    )(z, recv, down, up)


def weight_copies(rows, wq_hbm, wk_hbm, wv_hbm, wq_ref, wkv_ref, sems):
    copies = []
    for i, row in enumerate(rows):
        part = pl.ds(pl.multiple_of(row, 512), 512)
        copies.append(
            [
                pltpu.make_async_copy(wk_hbm.at[:, part], wkv_ref.at[i, 0:64], sems.at[0, i]),
                pltpu.make_async_copy(wv_hbm.at[:, part], wkv_ref.at[i, 64:128], sems.at[1, i]),
                pltpu.make_async_copy(wq_hbm.at[part], wq_ref.at[i], sems.at[2, i]),
            ]
        )
    for block in copies:
        for copy in block:
            copy.start()
    return copies


def add_blocks(hiddens, copies, wq_ref, wkv_ref, q, kv):
    for i, hidden in enumerate(hiddens):
        for copy in copies[i]:
            copy.wait()
        q = q + dot(hidden, wq_ref[i])
        kv = kv + dot_nt(hidden, wkv_ref[i])
    return q, kv


def base_kernel(
    place_ref, plan_hbm, h0_ref, h1_ref, ha_ref, hb_ref, h3_ref, wq_hbm, wk_hbm, wv_hbm, _,
    mine_ref, give_ref, wq_ref, wkv_ref, acc_ref, plan_ref, sems, plan_sem,
):
    y, z = place_ref[0], place_ref[1]
    rows = [(((y - a) & 3) * 4 + ((z - b) & 3)) * 512 for a in range(4) for b in range(4)]
    copies = weight_copies(rows, wq_hbm, wk_hbm, wv_hbm, wq_ref, wkv_ref, sems)
    plan_copy = pltpu.make_async_copy(plan_hbm, plan_ref, plan_sem)
    plan_copy.start()
    hiddens = [ref[b] for ref in (h0_ref, h1_ref) for b in range(4)]
    hiddens += [ha_ref[0], ha_ref[1], hb_ref[0], hb_ref[1]] + [h3_ref[b] for b in range(4)]
    q, kv = jnp.zeros((64, 512), F32), jnp.zeros((64, 128), F32)
    for i, hidden in enumerate(hiddens):
        for copy in copies[i]:
            copy.wait()
        q = q + dot(hidden, wq_ref[i])
        kv = kv + dot_nt(hidden, wkv_ref[i])
    parity = z & 1
    for c in range(5):
        cols = slice(c * 128, (c + 1) * 128)
        acc_ref[...] = q[:, cols] if c < 4 else kv
        even, odd = acc_ref[pl.ds(0, 32, 2), :], acc_ref[pl.ds(1, 32, 2), :]
        mine_ref[0:32, cols], give_ref[0:32, cols] = sides(parity, even, odd)
    plan_copy.wait()
    row = pl.ds(plan_ref[65] >> 1, 1)
    mine_ref[32:40, :] = jnp.broadcast_to(give_ref[row, :], (8, 640))
    give_ref[32:40, :] = jnp.broadcast_to(mine_ref[row, :], (8, 640))


def base_project(place, plan, bands, wq, wkt, wvt, after):
    return pl.pallas_call(
        base_kernel,
        out_shape=[
            jax.ShapeDtypeStruct((40, 640), F32),
            jax.ShapeDtypeStruct((40, 640), F32),
        ],
        in_specs=[SMEM, ANY] + [VMEM] * 5 + [ANY] * 4,
        out_specs=[VMEM] * 2,
        scratch_shapes=[
            pltpu.VMEM((16, 512, 512), BF16),
            pltpu.VMEM((16, 128, 512), BF16),
            pltpu.VMEM((64, 128), F32),
            pltpu.SMEM((66,), jnp.int32),
            pltpu.SemaphoreType.DMA((3, 16)),
            pltpu.SemaphoreType.DMA,
        ],
        cost_estimate=pl.CostEstimate(flops=671_000_000, bytes_accessed=11_700_000, transcendentals=0),
        compiler_params=pltpu.CompilerParams(vmem_limit_bytes=16 * 2**20),
        name="base_project",
    )(place, plan, *bands, *in_hbm(wq, wkt, wvt), after)


def rotate(part, cos, sin):
    return part * cos + pltpu.roll(part, 64, 1) * sin


def sides(parity, mine, other):
    even = parity == 0
    return jnp.where(even, mine, other), jnp.where(even, other, mine)


def project(parity, mine, other, low, cos, sin):
    def rounded(x):
        return x.astype(BF16).astype(F32)

    left, right = sides(parity, mine, other)
    heads = []
    for h in range(8):
        base = (left if h < 4 else right)[:, (h % 4) * 128 : (h % 4 + 1) * 128]
        heads.append(rounded(rotate(base + low[:, h * 128 : (h + 1) * 128], cos, sin)))
    key = jnp.concatenate([left[:, 512:576], right[:, 512:576]], axis=1) + low[:, 1024:1152]
    value = jnp.concatenate([left[:, 576:640], right[:, 576:640]], axis=1) + low[:, 1152:1280]
    return heads, rounded(rotate(key, cos, sin)), rounded(value)


def split(parity, outs, key, value):
    low = jnp.concatenate(outs[:4] + [key[:, :64], value[:, :64]], axis=1)
    high = jnp.concatenate(outs[4:] + [key[:, 64:], value[:, 64:]], axis=1)
    return sides(parity, low, high)


def attend_kernel(
    plan_ref, parity_ref, filled_ref, low_ref, mine_ref, other_ref, cos_ref, sin_ref, pair_ref, key_hbm, value_hbm,
    keep_ref, give_ref, rows_ref, query_ref, near_ref, fresh_ref, out_ref, key_ref, value_ref, sems,
):
    copies = []
    for g in range(4):
        hbm, ref = ((key_hbm, key_ref), (value_hbm, value_ref))[g // 2]
        part = pl.ds((g % 2) * 16, 16)
        copies.append(pltpu.make_async_copy(hbm.at[part], ref.at[part], sems.at[g]))
        copies[-1].start()
    parity = parity_ref[0]
    for i in range(32):
        rows_ref[i : i + 1, :] = low_ref[plan_ref[2 * i + parity]]
    rows_ref[32:40, :] = jnp.broadcast_to(low_ref[plan_ref[plan_ref[64]]], (8, 1280))
    last = plan_ref[65]

    def table(ref):
        mine = jnp.where(parity == 0, ref[pl.ds(0, 32, 2), :], ref[pl.ds(1, 32, 2), :])
        more = jnp.broadcast_to(ref[pl.ds(last, 1), :], (8, 128))
        return jnp.concatenate([mine, more], axis=0)

    heads, key, value = project(
        parity, mine_ref[...], other_ref[...], rows_ref[...], table(cos_ref), table(sin_ref)
    )
    for h in range(8):
        query_ref[pl.ds(h, 40, 8), :] = heads[h]
        near_ref[pl.ds(h, 40, 8), :] = key
        fresh_ref[pl.ds(h, 40, 8), :] = value
    scale = 1.0 / math.sqrt(HEAD)
    def caches(half, ref, which):
        return [ref[half * 16 + s] for s in range(16)] + ([pair_ref[which]] if half else [])

    halves = []
    for half in range(2):
        rows = slice(half * 128, half * 136 + 128)
        query = query_ref[rows, :]
        own = jnp.sum(query * near_ref[rows, :], axis=1, keepdims=True) * scale
        copies[half].wait()
        scores = jnp.concatenate(
            [
                dot_nt(query[s * 8 : s * 8 + 8].astype(BF16), block)
                for s, block in enumerate(caches(half, key_ref, 0))
            ],
            axis=0,
        ) * scale
        used = [filled_ref[2 * (half * 16 + s) + parity] for s in range(16)] + [filled_ref[last]] * half
        slot = lax.broadcasted_iota(jnp.int32, (8, 512), 1)
        left = jnp.concatenate([n - slot for n in used], axis=0)
        valid = left > 0
        top = jnp.max(jnp.where(valid, scores, -jnp.inf), axis=1, keepdims=True)
        top = jnp.maximum(top, own)
        weights = jnp.where(valid, jnp.exp(scores - top), 0.0)
        own_weight = jnp.exp(own - top)
        total = jnp.sum(weights, axis=1, keepdims=True) + own_weight
        halves.append((weights.astype(BF16), own_weight, total))
    for half in range(2):
        copies[2 + half].wait()
        weights, own_weight, total = halves[half]
        rows = slice(half * 128, half * 136 + 128)
        own = own_weight.astype(BF16).astype(F32) * fresh_ref[rows, :]
        out = jnp.concatenate(
            [
                dot(weights[s * 8 : s * 8 + 8], block)
                for s, block in enumerate(caches(half, value_ref, 1))
            ],
            axis=0,
        )
        out_ref[rows, :] = (out + own) / total
    outs = [out_ref[pl.ds(h, 40, 8), :] for h in range(8)]
    keep, give = split(parity, outs, key, value)
    keep_ref[...] = keep.astype(BF16)
    give_ref[...] = give.astype(BF16)


def attend_all(plan, parity, filled, low, mine, other, cos, sin, pair, keys, values):
    return pl.pallas_call(
        attend_kernel,
        out_shape=[jax.ShapeDtypeStruct((40, 640), BF16)] * 2,
        in_specs=[SMEM] * 3 + [VMEM] * 6 + [ANY] * 2,
        out_specs=[VMEM] * 2,
        scratch_shapes=[
            pltpu.VMEM((40, 1280), F32),
            pltpu.VMEM((320, 128), F32),
            pltpu.VMEM((320, 128), F32),
            pltpu.VMEM((320, 128), F32),
            pltpu.VMEM((320, 128), F32),
            pltpu.VMEM(keys.shape, BF16),
            pltpu.VMEM(values.shape, BF16),
            pltpu.SemaphoreType.DMA((4,)),
        ],
        cost_estimate=pl.CostEstimate(flops=70_000_000, bytes_accessed=1_000_000, transcendentals=131_072),
        compiler_params=pltpu.CompilerParams(vmem_limit_bytes=20 * 2**20),
        name="attend_all",
    )(plan, parity, filled, low, mine, other, cos, sin, pair, keys, values)


def weave_kernel(plan_ref, parity_ref, keep_ref, back_ref, out_ref, key_ref, value_ref, rows_ref, extra_ref):
    parity, first, last = parity_ref[0], plan_ref[64], plan_ref[65]
    keep, back = keep_ref[...].astype(F32), back_ref[...].astype(F32)
    even, odd = sides(parity, keep[0:32], back[0:32])
    extra_ref[...] = jnp.where(parity == (last & 1), back[32:40], keep[32:40])
    same = (first & 1) == (last & 1)
    for c in range(5):
        cols = slice(c * 128, (c + 1) * 128)
        rows_ref[pl.ds(0, 32, 2), :] = even[:, cols]
        rows_ref[pl.ds(1, 32, 2), :] = odd[:, cols]

        @pl.when(same)
        def _():
            rows_ref[pl.ds(last, 1), :] = extra_ref[0:1, cols]

        both = rows_ref[...].astype(BF16)
        if c < 4:
            out_ref[:, cols] = both
        else:
            key_ref[...] = both[:, 0:64]
            value_ref[...] = both[:, 64:128]


def weave(plan, parity, keep, back):
    return pl.pallas_call(
        weave_kernel,
        out_shape=[
            jax.ShapeDtypeStruct((64, 512), BF16),
            jax.ShapeDtypeStruct((64, 64), BF16),
            jax.ShapeDtypeStruct((64, 64), BF16),
        ],
        in_specs=[SMEM, SMEM, VMEM, VMEM],
        out_specs=[VMEM] * 3,
        scratch_shapes=[pltpu.VMEM((64, 128), F32), pltpu.VMEM((8, 640), F32)],
        compiler_params=pltpu.CompilerParams(vmem_limit_bytes=2 * 2**20),
        name="weave",
    )(plan, parity, keep, back)


def local(
    hidden, wq, wk, wv, down_maps, up_maps, key_cache, value_cache, filled, positions, requests, slots
):
    t = lax.axis_index("tensor")
    parity = t & 1
    z, y = t & 3, t >> 2
    swap = [(i, i ^ 1) for i in range(16)]

    def z_turn(k):
        return [(4 * a + b, 4 * a + (b + k) % 4) for a in range(4) for b in range(4)]

    def y_turn(k):
        return [(4 * a + b, 4 * ((a + k) % 4) + b) for a in range(4) for b in range(4)]

    plan, spread, code, down_near, up_near, hidden_near, pair = make_plan(
        z.reshape(1), requests, slots, hidden, down_maps.reshape(96, 8192), up_maps.reshape(32, 10240),
        key_cache[0], value_cache[0],
    )
    around_z = [hidden_near] + [lax.ppermute(hidden, "tensor", z_turn(k)) for k in (1, 2, 3)]
    sent = send_rows(spread, code, around_z)
    rings = [[g * 16 + a * 4 + b for a in range(4) for g in range(8)] for b in range(4)]
    recv = lax.all_to_all(sent, ("dp", "tensor"), 0, 0, tiled=True, axis_index_groups=rings)
    band = stack_band(plan, around_z)
    up, down = (lax.ppermute(band, "tensor", y_turn(k)) for k in (1, 3))

    halves = take_halves(up, down)
    halves = [lax.ppermute(half, "tensor", y_turn(k)) for half, k in zip(halves, (1, 3))]
    pair = lax.ppermute(pair, "tensor", swap)
    recv, up, down = lax.optimization_barrier((recv, up, down))
    low_sent = owner_low(z.reshape(1), recv, down_near, up_near)
    low_sent, pair, *halves = lax.optimization_barrier((low_sent, pair, *halves))
    low = lax.all_to_all(low_sent, ROUTE, 0, 0, tiled=True)

    place = jnp.stack([y, z]).astype(jnp.int32)
    mine, give = base_project(place, plan, (band, up, *halves, down), wq, wk.T, wv.T, low_sent)
    other = lax.ppermute(give, "tensor", swap)

    pos, mine = lax.optimization_barrier((positions, mine))
    freq = THETA ** (-2.0 * jnp.arange(64, dtype=F32) / HEAD)
    angle = pos.astype(F32)[:, None] * freq[None, :]
    cos, sin = jnp.cos(angle), jnp.sin(angle)
    cos, sin = jnp.concatenate([cos, cos], 1), jnp.concatenate([-sin, sin], 1)

    which = parity.reshape(1)
    keys, values = in_hbm(key_cache[0], value_cache[0])
    keep, give = attend_all(plan, which, filled, low, mine, other, cos, sin, pair, keys, values)
    back = lax.ppermute(give, "tensor", swap)
    return tuple(weave(plan, which, keep, back))


def solution(mesh):
    return jax.shard_map(
        local,
        mesh=mesh,
        in_specs=(
            P("dp", "tensor"),
            P(None, "tensor"),
            P(None, "tensor"),
            P(None, "tensor"),
            P(("dp", "tensor"), None, None),
            P(("dp", "tensor"), None, None),
            P("tensor", "dp", None, None),
            P("tensor", "dp", None, None),
            P("dp"),
            P("dp"),
            P("dp", None),
            P("dp"),
        ),
        out_specs=(P("dp", "tensor"), P("dp", "tensor"), P("dp", "tensor")),
        check_vma=False,
    )
```
